256 devices in a mesh: seq: 16 (over y, x), exp: 16 (over z, core).
Axes of the slice: x: 4, y: 4, z: 8, core: 2. Of those that a mesh axis runs over, the one named last changes fastest.
Arguments:
- enc_in: bfloat16 [16, 4096, 1024], P('exp', 'seq'), may hold values from -6 to 6
- expert_ids: int32 [16, 4096], P('exp', 'seq'), may hold values from 0 to 63, as said below
- slots: int32 [16, 4096], P('exp', 'seq'), may hold values from 0 to 4, as said below
- expert_gate: float32 [16, 4096], P('exp', 'seq'), may hold values from 0.2 to 1
- moe_gain: float32 [1024], replicated, may hold values from 0.25 to 1.75
- w_in: bfloat16 [64, 1024, 2816], P('exp', None, 'seq'), may hold values from -0.1875 to 0.1875
- w_out: bfloat16 [64, 2816, 1024], P('exp', 'seq'), may hold values from -0.109375 to 0.109375
- final_gain: float32 [1024], replicated, may hold values from 0.25 to 1.75
- w_key: bfloat16 [1024, 1024], replicated, may hold values from -0.1875 to 0.1875
- w_value: bfloat16 [1024, 1024], replicated, may hold values from -0.1875 to 0.1875
- dec_query: bfloat16 [16, 2048, 1024], P('exp', 'seq'), may hold values from -400 to 400
Outputs:
- enc_out: bfloat16 [16, 4096, 1024], P('exp', 'seq')
- context: bfloat16 [16, 2048, 1024], P('exp', 'seq')
The draws below stay inside these ranges and needn't reach their ends.
Inputs may be any that keep to these rules, and one draw needn't show every extreme that they name: `expert_ids`: in every device block of 256 consecutive tokens of a document, some expert is named by more than 4 tokens. slots of a token is the number of earlier tokens of its device block of 256 tokens that name the same expert, or 4 if that number is 4 or more (the token is dropped).
All inputs are finite; a program needn't handle non-finite values.
Results may differ from the reference program's by a relative error of at most 0.039.
Values may be sent and summed in bfloat16 or wider, within the bound.
A program may use at most 128 MiB of HBM per device.

```python
import jax
import jax.numpy as jnp
from jax import lax

D = 1024
FF = 2816
HEADS = 16
TOK_DEV = 256
EXPERTS = 64
DOCS = 16
ENC = 4096
DEC = 2048


def route_table(key):
    blocks = DOCS * ENC // TOK_DEV
    hot_expert = jax.random.randint(jax.random.fold_in(key, 5), (), 0, EXPERTS)
    chosen = jax.random.randint(jax.random.fold_in(key, 6), (blocks, TOK_DEV), 0, EXPERTS)
    raw = jax.random.randint(jax.random.fold_in(key, 7), (blocks, TOK_DEV), 0, 1 << 20)
    scores = raw * TOK_DEV + jnp.arange(TOK_DEV, dtype=jnp.int32)[None, :]
    order = jnp.argsort(scores, axis=1)
    ranked = jnp.argsort(order, axis=1)
    capacity = TOK_DEV // EXPERTS
    chosen = jnp.where(ranked <= capacity, hot_expert, chosen)
    return chosen.astype(jnp.int32)


def draw_expert_ids(key, part):
    return route_table(key).reshape(DOCS, ENC)


def draw_slots(key, part):
    chosen = route_table(key)
    capacity = TOK_DEV // EXPERTS
    same = chosen[:, :, None] == chosen[:, None, :]
    positions = jnp.arange(TOK_DEV, dtype=jnp.int32)
    earlier = positions[None, :] < positions[:, None]
    counted = jnp.sum((same & earlier[None, :, :]).astype(jnp.int32), axis=2)
    return jnp.minimum(counted, capacity).astype(jnp.int32).reshape(DOCS, ENC)


def draw_dec_query(key, part):
    key = jax.random.fold_in(key, 11)
    first_key = jax.random.fold_in(key, 0)
    base = jnp.clip(jax.random.normal(first_key, (DOCS, DEC, D), jnp.float32), -6.0, 6.0)
    return base.astype(jnp.bfloat16)


def levels(key, shape, pieces, least, top_value):
    def one(dim, blocks):
        steps = jax.random.uniform(jax.random.fold_in(jax.random.fold_in(key, 6), dim), (blocks,), jnp.float32, least / len(pieces), top_value / len(pieces))
        return jnp.repeat(jnp.exp(steps), shape[dim] // blocks).reshape((-1,) + (1,) * (len(shape) - dim - 1))

    level = one(*pieces[0])
    for cut in pieces[1:]:
        level = level * one(*cut)
    return level


def gaussian(key, extent, scale, most, cuts=(), kind=jnp.bfloat16):
    entries = scale * jax.random.normal(key, extent, jnp.float32)
    if cuts:
        entries = entries * levels(key, extent, cuts, -0.22, 0.18)
    return jnp.clip(entries, -most, most).astype(kind)


def setup_inputs(seed: int = 0) -> dict:
    seeds = jax.random.split(jax.random.key(seed), 12)
    enc_in = gaussian(seeds[0], (DOCS, ENC, D), 1.0, 6.0, ((0, 16), (1, 16)))
    expert_ids = draw_expert_ids(jax.random.fold_in(seeds[11], 71), 0)
    slots = draw_slots(jax.random.fold_in(seeds[11], 71), 0)
    expert_gate = jnp.clip(0.2 + 0.8 * jax.random.uniform(seeds[3], (DOCS, ENC), jnp.float32) ** levels(seeds[3], (DOCS, ENC), ((0, 16), (1, 16)), -0.2, 0.2), 0.2, 1.0)
    moe_gain = jnp.clip(1.0 + 0.15 * jax.random.normal(seeds[4], (D,), jnp.float32), 0.25, 1.75)
    w_in = gaussian(seeds[5], (EXPERTS, D, FF), D ** -0.5, 0.1875, ((0, 16), (2, 16)))
    w_out = gaussian(seeds[6], (EXPERTS, FF, D), FF ** -0.5, 0.109375, ((0, 16), (1, 16)))
    final_gain = jnp.clip(1.0 + 0.15 * jax.random.normal(seeds[7], (D,), jnp.float32), 0.25, 1.75)
    w_key = gaussian(seeds[8], (D, D), D ** -0.5, 0.1875)
    w_value = gaussian(seeds[9], (D, D), D ** -0.5, 0.1875)
    dec_query = draw_dec_query(jax.random.fold_in(seeds[11], 71), 0)
    return dict(enc_in=enc_in, expert_ids=expert_ids, slots=slots, expert_gate=expert_gate, moe_gain=moe_gain, w_in=w_in, w_out=w_out, final_gain=final_gain, w_key=w_key, w_value=w_value, dec_query=dec_query)


def rms_scale(values, gain):
    mean_square = lax.optimization_barrier(jnp.mean(values * values, axis=-1, keepdims=True))
    return values * lax.rsqrt(mean_square + 1e-06) * gain

def reference(enc_in, expert_ids, slots, expert_gate, moe_gain, w_in, w_out, final_gain, w_key, w_value, dec_query):
    width = enc_in.shape[2]
    capacity = TOK_DEV // EXPERTS
    total = DOCS * ENC
    blocks = total // TOK_DEV
    inputs = enc_in.astype(jnp.float32).reshape(total, width)
    normed = rms_scale(inputs, moe_gain.astype(jnp.float32)).astype(jnp.bfloat16)
    route = expert_ids.reshape(total).astype(jnp.int32)
    slot_pos = slots.reshape(total).astype(jnp.int32)
    kept = slot_pos < capacity
    block_of = (jnp.arange(total, dtype=jnp.int32) // TOK_DEV).astype(jnp.int32)
    column = jnp.where(kept, block_of * capacity + slot_pos, blocks * capacity).astype(jnp.int32)
    buffers = jnp.zeros((EXPERTS, blocks * capacity, width), jnp.bfloat16)
    buffers = buffers.at[route, column].set(normed, mode='drop')

    def expert_ffn(operands):
        tokens, first_w, second_w = operands
        hidden = jnp.maximum(jnp.dot(tokens, first_w, preferred_element_type=jnp.float32), 0.0).astype(jnp.bfloat16)
        return jnp.dot(hidden, second_w, preferred_element_type=jnp.float32).astype(jnp.bfloat16)
    outputs = lax.map(expert_ffn, (buffers, w_in, w_out))
    picked = outputs[route, jnp.minimum(column, blocks * capacity - 1)].astype(jnp.float32)
    moe = jnp.where(kept[:, None], picked, 0.0)
    enc_rows = inputs + expert_gate.reshape(total, 1).astype(jnp.float32) * moe
    enc_out = enc_rows.astype(jnp.bfloat16).reshape(DOCS, ENC, width)
    head_dim = width // HEADS
    factor = head_dim ** (-0.5)

    def attend(operands):
        enc_doc, query_doc = operands
        normed_doc = rms_scale(enc_doc.astype(jnp.float32), final_gain.astype(jnp.float32)).astype(jnp.bfloat16)
        keys = jnp.dot(normed_doc, w_key, preferred_element_type=jnp.float32).astype(jnp.bfloat16)
        values = jnp.dot(normed_doc, w_value, preferred_element_type=jnp.float32).astype(jnp.bfloat16)
        q_heads = query_doc.astype(jnp.float32).reshape(DEC, HEADS, head_dim)
        k_heads = keys.astype(jnp.float32).reshape(ENC, HEADS, head_dim)
        v_heads = values.astype(jnp.float32).reshape(ENC, HEADS, head_dim)
        scores = jnp.einsum('qhd,khd->hqk', q_heads, k_heads) * factor
        top = lax.optimization_barrier(jnp.max(scores, axis=-1, keepdims=True))
        expo = jnp.exp(scores - top)
        totals = lax.optimization_barrier(jnp.sum(expo, axis=-1))
        rounded = lax.optimization_barrier(expo.astype(jnp.bfloat16))
        weights = rounded.astype(jnp.float32)
        numer = jnp.einsum('hqk,khd->qhd', weights, v_heads)
        result = numer / jnp.transpose(totals)[:, :, None]
        return result.reshape(DEC, width).astype(jnp.bfloat16)
    context = lax.map(attend, (enc_out, dec_query))
    return (enc_out, context)
```

```python
import functools

import jax
import jax.numpy as jnp
from jax import lax
from jax.experimental import pallas as pl
from jax.experimental.pallas import tpu as pltpu
from jax.sharding import PartitionSpec as P

HEADS = 16
MESH = pl.DeviceIdType.MESH
F32 = jnp.float32
BF16 = jnp.bfloat16


def rms_scale(values, gain):
    mean_square = jnp.mean(values * values, axis=-1, keepdims=True)
    return values * lax.rsqrt(mean_square + 1e-06) * gain


def rows_at(index, count):
    return pl.ds(pl.multiple_of(index * count, count), count)


def greet(axes):
    barrier = pltpu.get_barrier_semaphore()
    total = 0
    for axis in axes:
        n = lax.axis_size(axis)
        me = lax.axis_index(axis)
        total += n - 1

        def signal(d, carry, axis=axis, n=n, me=me):
            pl.semaphore_signal(
                barrier, inc=1, device_id={axis: lax.rem(me + d, n)}, device_id_type=MESH
            )
            return carry

        lax.fori_loop(1, n, signal, 0)
    pl.semaphore_wait(barrier, total)


class Exchange:
    def __init__(self, axis, source, landing, send, recv):
        self.axis, self.source, self.landing = axis, source, landing
        self.send, self.recv = send, recv
        self.n, self.me = lax.axis_size(axis), lax.axis_index(axis)

    def copy(self, d, slot):
        t = lax.rem(self.me + d, self.n)
        return pltpu.make_async_remote_copy(
            src_ref=self.source(t),
            dst_ref=self.landing(slot),
            send_sem=self.send.at[d],
            recv_sem=self.recv.at[d],
            device_id={self.axis: t},
            device_id_type=MESH,
        )

    def start_one(self, d):
        self.copy(d, self.me).start()

    def wait_one(self, d):
        self.copy(d, lax.rem(self.me + self.n - d, self.n)).wait_recv()

    def loop(self, act):
        def body(d, carry):
            act(d)
            return carry

        lax.fori_loop(1, self.n, body, 0)

    def start(self):
        self.loop(self.start_one)

    def arrived(self):
        self.loop(self.wait_one)

    def sent(self):
        self.loop(lambda d: self.copy(d, self.me).wait_send())


def moe_kernel(
    packed_ref,
    win_ref,
    wout_ref,
    q_ref,
    back_ref,
    qland_ref,
    zland,
    rows,
    rland,
    win_land,
    wout_land,
    part,
    pland,
    brows,
    zback,
    bland,
    qsend,
    local_sem,
    z_send,
    z_recv,
    wi_send,
    wi_recv,
    wo_send,
    wo_recv,
    r_send,
    r_recv,
    p_send,
    p_recv,
    b_send,
    b_recv,
    q_send,
    q_recv,
):
    seq, exp = lax.axis_index("seq"), lax.axis_index("exp")
    n_seq = lax.axis_size("seq")
    experts = win_ref.shape[0]
    share = n_seq // experts
    my_y, my_x = seq // share, lax.rem(seq, share)
    zrows = packed_ref.shape[0] // lax.axis_size("exp")
    srows = packed_ref.shape[0] // experts
    greet(("seq", "exp"))

    z_out = Exchange(
        "exp",
        lambda t: packed_ref.at[rows_at(t, zrows)],
        lambda s: zland.at[rows_at(s, zrows)],
        z_send,
        z_recv,
    )
    z_out.start()
    zland[rows_at(exp, zrows), :] = packed_ref[rows_at(exp, zrows), :]

    def weight_copy(d, slot, ref, land, send, recv):
        k = lax.rem(my_y + d, experts)
        return pltpu.make_async_remote_copy(
            src_ref=ref.at[k],
            dst_ref=land.at[slot],
            send_sem=send.at[d],
            recv_sem=recv.at[d],
            device_id={"seq": k * share + my_x},
            device_id_type=MESH,
        )

    weights = ((win_ref, win_land, wi_send, wi_recv), (wout_ref, wout_land, wo_send, wo_recv))
    for d in range(1, experts):
        for each in weights:
            weight_copy(d, my_y, *each).start()
    own = [
        pltpu.make_async_copy(ref.at[my_y], land.at[my_y], local_sem.at[i])
        for i, (ref, land, _, _) in enumerate(weights)
    ]
    for copy in own:
        copy.start()

    lane = lax.broadcasted_iota(jnp.int32, (q_ref.shape[0], 128), 1)
    for p in range(HEADS // 2):
        pair = pltpu.roll(q_ref[:, p * 128 : (p + 1) * 128].astype(F32) * 0.125, 64, 1)
        qsend[2 * p] = jnp.where(lane >= 64, pair, 0.0).astype(BF16)
        qsend[2 * p + 1] = jnp.where(lane < 64, pair, 0.0).astype(BF16)
    q_out = Exchange(
        "seq", lambda t: qsend.at[t], lambda s: qland_ref.at[s], q_send, q_recv
    )
    q_own = pltpu.make_async_copy(qsend.at[seq], qland_ref.at[seq], local_sem.at[2])
    q_own.start()

    total = packed_ref.shape[0]
    capacity = zrows // experts
    out_row = lax.broadcasted_iota(jnp.int32, (total, total), 0)
    in_row = lax.broadcasted_iota(jnp.int32, (total, total), 1)

    def by_expert(r):
        j, k, c = r // zrows, lax.rem(r // capacity, experts), lax.rem(r, capacity)
        return k * srows + j * capacity + c

    forward = (by_expert(in_row) == out_row).astype(BF16)
    inverse = (by_expert(out_row) == in_row).astype(BF16)

    z_out.arrived()
    rows[...] = jnp.dot(forward, zland[...], preferred_element_type=F32).astype(BF16)

    r_out = Exchange(
        "seq",
        lambda t: rows.at[rows_at(t // share, srows)],
        lambda s: rland.at[rows_at(s, srows)],
        r_send,
        r_recv,
    )
    r_out.start()
    q_out.start()
    rland[rows_at(seq, srows), :] = rows[rows_at(my_y, srows), :]
    for copy in own:
        copy.wait()
    for d in range(1, experts):
        slot = lax.rem(my_y + experts - d, experts)
        for each in weights:
            weight_copy(d, slot, *each).wait_recv()
    r_out.arrived()

    tile = 256

    def ffn(m, carry):
        block = rland[rows_at(m, tile), :]
        acc = None
        for h in range(experts):
            product = jnp.dot(block, win_land[h], preferred_element_type=F32)
            hidden = jnp.maximum(product, 0.0).astype(BF16)
            term = jnp.dot(hidden, wout_land[h], preferred_element_type=F32)
            acc = term if acc is None else acc + term
        part[rows_at(m, tile), :] = acc
        return carry

    lax.fori_loop(0, rland.shape[0] // tile, ffn, 0)

    p_out = Exchange(
        "seq",
        lambda t: part.at[rows_at(t, srows)],
        lambda s: pland.at[s],
        p_send,
        p_recv,
    )
    p_out.start()
    pland[seq] = part[rows_at(seq, srows), :]
    p_out.arrived()
    for k in range(experts):
        acc = pland[k * share]
        for i in range(1, share):
            acc = acc + pland[k * share + i]
        brows[k * srows : (k + 1) * srows, :] = acc.astype(BF16)
    zback[...] = jnp.dot(inverse, brows[...], preferred_element_type=F32).astype(BF16)

    b_out = Exchange(
        "exp",
        lambda t: zback.at[rows_at(t, zrows)],
        lambda s: bland.at[rows_at(s, zrows)],
        b_send,
        b_recv,
    )
    b_out.start()
    bland[rows_at(exp, zrows), :] = zback[rows_at(exp, zrows), :]
    q_own.wait()
    q_out.arrived()
    b_out.arrived()
    back_ref[...] = bland[...]
    for exchange in (z_out, r_out, q_out, p_out, b_out):
        exchange.sent()
    for d in range(1, experts):
        for each in weights:
            weight_copy(d, my_y, *each).wait_send()


def attend_kernel(
    rows_ref,
    wk_ref,
    wv_ref,
    q_ref,
    out_ref,
    kvsend,
    kvland,
    csend,
    cland,
    k_send,
    k_recv,
    c_send,
    c_recv,
):
    seq = lax.axis_index("seq")
    n_seq = lax.axis_size("seq")
    count = rows_ref.shape[0]
    greet(("seq",))
    lane = lax.broadcasted_iota(jnp.int32, (count, 128), 1)
    low = lane < 64
    block = rows_ref[...]
    for g in range(HEADS // 4):
        cols = slice(g * 256, (g + 1) * 256)
        keys = jnp.dot(block, wk_ref[:, cols], preferred_element_type=F32)
        values = jnp.dot(block, wv_ref[:, cols], preferred_element_type=F32)
        for i in range(2):
            k_pair = pltpu.roll(keys[:, i * 128 : (i + 1) * 128], 64, 1)
            v_pair = values[:, i * 128 : (i + 1) * 128]
            head = g * 4 + i * 2
            kvsend[head] = jnp.where(low, v_pair, k_pair).astype(BF16)
            kvsend[head + 1] = jnp.where(low, k_pair, v_pair).astype(BF16)
    kv_out = Exchange(
        "seq",
        lambda t: kvsend.at[t],
        lambda s: kvland.at[rows_at(s, count)],
        k_send,
        k_recv,
    )
    kv_out.start()
    kvland[rows_at(seq, count), :] = kvsend[seq]
    kv_out.arrived()

    c_out = Exchange("seq", lambda t: csend.at[t], lambda s: cland.at[s], c_send, c_recv)

    def attend(t):
        kv = kvland[...]
        scores = lax.dot_general(
            q_ref[t], kv, (((1,), (1,)), ((), ())), preferred_element_type=F32
        )
        expo = jnp.exp(scores - jnp.max(scores, axis=-1, keepdims=True))
        total = jnp.sum(expo, axis=-1, keepdims=True)
        mixed = jnp.dot(expo.astype(BF16), kv, preferred_element_type=F32)
        return (mixed / total).astype(BF16)

    def step(d, carry):
        t = lax.rem(seq + d, n_seq)
        csend[t] = attend(t)
        c_out.start_one(d)
        return carry

    lax.fori_loop(1, n_seq, step, 0)
    cland[seq] = attend(seq)
    c_out.arrived()
    low = lax.broadcasted_iota(jnp.int32, cland.shape[1:], 1) < 64
    for p in range(HEADS // 2):
        out_ref[:, p * 128 : (p + 1) * 128] = jnp.where(low, cland[2 * p], cland[2 * p + 1])
    kv_out.sent()
    c_out.sent()


def per_device(
    enc_in,
    expert_ids,
    slots,
    expert_gate,
    moe_gain,
    w_in,
    w_out,
    final_gain,
    w_key,
    w_value,
    dec_query,
):
    n_exp, n_seq = lax.axis_size("exp"), lax.axis_size("seq")
    tok_rows, width = enc_in.shape[1:]
    experts, _, part_ff = w_in.shape
    capacity = tok_rows // (experts * n_exp)
    srows = tok_rows // experts
    q_rows = dec_query.shape[1]
    inputs = enc_in[0].astype(F32)
    normed = rms_scale(inputs, moe_gain).astype(BF16)
    kept = slots[0] < capacity
    target = jnp.where(kept, expert_ids[0] * capacity + slots[0], -1)
    places = jnp.arange(tok_rows, dtype=jnp.int32)
    dispatch = (places[:, None] == target[None, :]).astype(BF16)
    combine = (target[:, None] == places[None, :]).astype(BF16)
    packed = jnp.dot(dispatch, normed, preferred_element_type=F32).astype(BF16)

    vmem = pl.BlockSpec(memory_space=pltpu.VMEM)
    hbm = pl.BlockSpec(memory_space=pl.ANY)
    dma = pltpu.SemaphoreType.DMA
    back, queries = pl.pallas_call(
        moe_kernel,
        out_shape=(
            jax.ShapeDtypeStruct((tok_rows, width), BF16),
            jax.ShapeDtypeStruct((n_seq, q_rows, 128), BF16),
        ),
        in_specs=[vmem, hbm, hbm, vmem],
        out_specs=(vmem, hbm),
        scratch_shapes=[
            pltpu.VMEM((tok_rows, width), BF16),
            pltpu.VMEM((tok_rows, width), BF16),
            pltpu.VMEM((n_seq * srows, width), BF16),
            pltpu.VMEM((experts, width, part_ff), BF16),
            pltpu.VMEM((experts, part_ff, width), BF16),
            pltpu.VMEM((n_seq * srows, width), F32),
            pltpu.VMEM((n_seq, srows, width), F32),
            pltpu.VMEM((tok_rows, width), BF16),
            pltpu.VMEM((tok_rows, width), BF16),
            pltpu.VMEM((tok_rows, width), BF16),
            pltpu.VMEM((n_seq, q_rows, 128), BF16),
            dma((3,)),
            dma((n_exp,)),
            dma((n_exp,)),
            dma((experts,)),
            dma((experts,)),
            dma((experts,)),
            dma((experts,)),
        ]
        + [dma((n_seq,))] * 4
        + [dma((n_exp,))] * 2
        + [dma((n_seq,))] * 2,
        compiler_params=pltpu.CompilerParams(
            collective_id=0, has_side_effects=True, vmem_limit_bytes=40 << 20
        ),
        name="experts",
    )(packed, w_in, w_out, dec_query[0])

    combined = jnp.dot(combine, back, preferred_element_type=F32)
    enc_rows = inputs + expert_gate[0][:, None] * combined
    enc_out = enc_rows.astype(BF16)
    kv_rows = rms_scale(enc_out.astype(F32), final_gain).astype(BF16)
    context = pl.pallas_call(
        attend_kernel,
        out_shape=jax.ShapeDtypeStruct((q_rows, width), BF16),
        in_specs=[vmem] * 4,
        out_specs=vmem,
        scratch_shapes=[
            pltpu.VMEM((n_seq, tok_rows, 128), BF16),
            pltpu.VMEM((n_seq * tok_rows, 128), BF16),
            pltpu.VMEM((n_seq, q_rows, 128), BF16),
            pltpu.VMEM((n_seq, q_rows, 128), BF16),
        ]
        + [dma((n_seq,))] * 4,
        compiler_params=pltpu.CompilerParams(
            collective_id=1, has_side_effects=True, vmem_limit_bytes=40 << 20
        ),
        name="attend",
    )(kv_rows, w_key, w_value, queries)
    return (enc_out[None], context[None])


def solution(mesh):
    placed = (
        P("exp", "seq", None),
        P("exp", "seq"),
        P("exp", "seq"),
        P("exp", "seq"),
        P(),
        P("exp", None, "seq"),
        P("exp", "seq", None),
        P(),
        P(),
        P(),
        P("exp", "seq", None),
    )
    return jax.shard_map(
        per_device,
        mesh=mesh,
        in_specs=placed,
        out_specs=(P("exp", "seq", None), P("exp", "seq", None)),
        check_vma=False,
    )
```

```python
import functools

import jax
import jax.numpy as jnp
from jax import lax
from jax.experimental import pallas as pl
from jax.experimental.pallas import tpu as pltpu
from jax.sharding import PartitionSpec as P

HEADS = 16
MESH = pl.DeviceIdType.MESH
F32 = jnp.float32
BF16 = jnp.bfloat16


def rms_scale(values, gain):
    mean_square = jnp.mean(values * values, axis=-1, keepdims=True)
    return values * lax.rsqrt(mean_square + 1e-06) * gain


def rows_at(index, count):
    return pl.ds(pl.multiple_of(index * count, count), count)


def signal_all(axes):
    barrier = pltpu.get_barrier_semaphore()
    total = 0
    for axis in axes:
        n = lax.axis_size(axis)
        me = lax.axis_index(axis)
        total += n - 1

        def signal(d, carry, axis=axis, n=n, me=me):
            pl.semaphore_signal(
                barrier, inc=1, device_id={axis: lax.rem(me + d, n)}, device_id_type=MESH
            )
            return carry

        lax.fori_loop(1, n, signal, 0)
    return barrier, total


class Exchange:
    def __init__(self, axis, source, landing, send, recv):
        self.axis, self.source, self.landing = axis, source, landing
        self.send, self.recv = send, recv
        self.n, self.me = lax.axis_size(axis), lax.axis_index(axis)

    def copy(self, d, slot):
        t = lax.rem(self.me + d, self.n)
        return pltpu.make_async_remote_copy(
            src_ref=self.source(t),
            dst_ref=self.landing(slot),
            send_sem=self.send.at[d],
            recv_sem=self.recv.at[d],
            device_id={self.axis: t},
            device_id_type=MESH,
        )

    def start_one(self, d):
        self.copy(d, self.me).start()

    def wait_one(self, d):
        self.copy(d, lax.rem(self.me + self.n - d, self.n)).wait_recv()

    def loop(self, act):
        def body(d, carry):
            act(d)
            return carry

        lax.fori_loop(1, self.n, body, 0)

    def start(self):
        self.loop(self.start_one)

    def arrived(self):
        self.loop(self.wait_one)

    def sent(self):
        self.loop(lambda d: self.copy(d, self.me).wait_send())


def remote(src, dst, send, recv, seq):
    return pltpu.make_async_remote_copy(
        src_ref=src,
        dst_ref=dst,
        send_sem=send,
        recv_sem=recv,
        device_id={"seq": seq},
        device_id_type=MESH,
    )


def moe_kernel(
    enc_ref,
    ids_ref,
    slots_ref,
    gain_ref,
    win_ref,
    wout_ref,
    q_ref,
    back_ref,
    qland_ref,
    enc,
    query,
    packed,
    zland,
    rows,
    rland,
    win_land,
    wout_land,
    part,
    half_up,
    half_down,
    full_up,
    full_down,
    brows,
    gback,
    zback,
    bland,
    qsend,
    local_sem,
    z_send,
    z_recv,
    b_send,
    b_recv,
    q_send,
    q_recv,
    wi_send,
    wi_recv,
    wo_send,
    wo_recv,
    g_send,
    g_recv,
    up_send,
    up_recv,
    down_send,
    down_recv,
    fwd_send,
    fwd_recv,
    h_send,
    h_recv,
    f_send,
    f_recv,
    gb_send,
    gb_recv,
):
    seq, exp = lax.axis_index("seq"), lax.axis_index("exp")
    n_seq, n_exp = lax.axis_size("seq"), lax.axis_size("exp")
    experts = win_ref.shape[0]
    hidden_part = win_ref.shape[1]
    tok = enc_ref.shape[0]
    zrows, srows = tok // n_exp, tok // experts
    capacity = zrows // experts
    core = lax.rem(exp, 2)
    y, x = seq // experts, lax.rem(seq, experts)
    line, rank = y + core * (x - y), x + core * (y - x)

    def at(g, r):
        return g * (experts - core * (experts - 1)) + r * (1 + core * (experts - 1))

    def turn(value, d):
        return lax.rem(value + experts + d, experts)

    enc_in = pltpu.make_async_copy(enc_ref, enc, local_sem.at[0])
    q_in = pltpu.make_async_copy(q_ref, query, local_sem.at[1])
    enc_in.start()
    q_in.start()
    barrier, greeted = signal_all(("seq", "exp"))
    own_weights = [
        pltpu.make_async_copy(
            ref.at[line], land.at[rows_at(line, hidden_part)], local_sem.at[2 + i]
        )
        for i, (ref, land) in enumerate(((win_ref, win_land), (wout_ref, wout_land)))
    ]
    for copy in own_weights:
        copy.start()
    enc_in.wait()
    normed = rms_scale(enc[...].astype(F32), gain_ref[...]).astype(BF16)
    target = jnp.where(slots_ref[...] < capacity, ids_ref[...] * capacity + slots_ref[...], -1)
    out_row = lax.broadcasted_iota(jnp.int32, (tok, tok), 0)
    in_row = lax.broadcasted_iota(jnp.int32, (tok, tok), 1)
    dispatch = (out_row == target).astype(BF16)
    packed[...] = jnp.dot(dispatch, normed, preferred_element_type=F32).astype(BF16)
    pl.semaphore_wait(barrier, greeted)

    z_out = Exchange(
        "exp",
        lambda t: packed.at[rows_at(t, zrows)],
        lambda s: zland.at[rows_at(s, zrows)],
        z_send,
        z_recv,
    )
    z_out.start()

    def weight_copy(d, slot, ref, land, send, recv):
        k = turn(line, d)
        return remote(
            ref.at[k], land.at[rows_at(slot, hidden_part)], send.at[d], recv.at[d], at(k, rank)
        )

    weights = ((win_ref, win_land, wi_send, wi_recv), (wout_ref, wout_land, wo_send, wo_recv))
    for each in weights:
        for d in range(1, experts):
            weight_copy(d, line, *each).start()
    zland[rows_at(exp, zrows), :] = packed[rows_at(exp, zrows), :]

    q_in.wait()
    lane = lax.broadcasted_iota(jnp.int32, (q_ref.shape[0], 128), 1)
    for p in range(HEADS // 2):
        pair = pltpu.roll(query[:, p * 128 : (p + 1) * 128].astype(F32) * 0.125, 64, 1)
        qsend[2 * p] = jnp.where(lane >= 64, pair, 0.0).astype(BF16)
        qsend[2 * p + 1] = jnp.where(lane < 64, pair, 0.0).astype(BF16)
    q_out = Exchange(
        "seq", lambda t: qsend.at[t], lambda s: qland_ref.at[s], q_send, q_recv
    )
    q_own = pltpu.make_async_copy(qsend.at[seq], qland_ref.at[seq], local_sem.at[0])
    q_own.start()

    def by_expert(r):
        j, k, c = r // zrows, lax.rem(r // capacity, experts), lax.rem(r, capacity)
        return k * srows + j * capacity + c

    forward = (by_expert(in_row) == out_row).astype(BF16)
    inverse = (by_expert(out_row) == in_row).astype(BF16)
    z_out.arrived()
    rows[...] = jnp.dot(forward, zland[...], preferred_element_type=F32).astype(BF16)

    def piece(r, g):
        return rland.at[r, rows_at(g, srows)]

    def to_line(d, slot):
        k = turn(line, d)
        return remote(
            rows.at[rows_at(k, srows)], piece(rank, slot), g_send.at[d], g_recv.at[d], at(k, rank)
        )

    def up(d, r):
        g = turn(line, -d)
        return remote(
            piece(rank, g), piece(r, g), up_send.at[d], up_recv.at[d], at(line, turn(rank, 1))
        )

    def down(d, r):
        g = turn(line, -d)
        return remote(
            piece(rank, g), piece(r, g), down_send.at[d], down_recv.at[d], at(line, turn(rank, -1))
        )

    def forwarded(d, r):
        g = turn(line, -d)
        way = 1 if d < 2 else -1
        return remote(
            piece(turn(rank, -way), g),
            piece(r, g),
            fwd_send.at[d],
            fwd_recv.at[d],
            at(line, turn(rank, way)),
        )

    for d in range(1, experts):
        to_line(d, line).start()
    rland[rank, rows_at(line, srows), :] = rows[rows_at(line, srows), :]
    for d in range(experts):
        if d:
            to_line(d, turn(line, -d)).wait_recv()
        up(d, rank).start()
        down(d, rank).start()
    for copy in own_weights:
        copy.wait()
    for d in range(1, experts):
        for each in weights:
            weight_copy(d, turn(line, -d), *each).wait_recv()

    def ffn(r):
        product = lax.dot_general(
            rland[r], win_land[...], (((1,), (1,)), ((), ())), preferred_element_type=F32
        )
        hidden = jnp.maximum(product, 0.0).astype(BF16)
        part[r] = jnp.dot(hidden, wout_land[...], preferred_element_type=F32)

    above, below, across = turn(rank, 1), turn(rank, -1), turn(rank, 2)
    for d in (0, 1):
        up(d, below).wait_recv()
        forwarded(d, below).start()
    ffn(rank)
    for d in (2, 3):
        down(d, above).wait_recv()
        forwarded(d, above).start()
    for d in (2, 3):
        up(d, below).wait_recv()
    ffn(below)
    for d in (0, 1):
        down(d, above).wait_recv()
    ffn(above)
    for d in range(experts):
        forwarded(d, across).wait_recv()
    ffn(across)

    mid = tok // 2
    first, second = pl.ds(0, mid), pl.ds(mid, mid)
    far_up = remote(
        part.at[across, first], half_up, h_send.at[0], h_recv.at[0], at(line, above)
    )
    far_down = remote(
        part.at[across, second], half_down, h_send.at[1], h_recv.at[1], at(line, below)
    )
    near = [
        remote(part.at[r, rows_], land.at[rows_], f_send.at[i], f_recv.at[i], at(line, r))
        for i, (r, rows_, land) in enumerate(
            (
                (above, second, full_up),
                (below, first, full_down),
                (above, first, full_up),
                (below, second, full_down),
            )
        )
    ]
    far_up.start()
    far_down.start()
    near[0].start()
    near[1].start()
    far_up.wait_recv()
    part[above, first, :] = part[above, first, :] + half_up[...]
    near[2].start()
    far_down.wait_recv()
    part[below, second, :] = part[below, second, :] + half_down[...]
    near[3].start()
    near[0].wait_recv()
    near[3].wait_recv()
    brows[second, :] = (part[rank, second, :] + full_up[second, :] + full_down[second, :]).astype(
        BF16
    )
    near[1].wait_recv()
    near[2].wait_recv()
    brows[first, :] = (part[rank, first, :] + full_up[first, :] + full_down[first, :]).astype(BF16)

    def from_line(d, slot):
        g = turn(line, d)
        return remote(
            brows.at[rows_at(g, srows)],
            gback.at[rows_at(slot, srows)],
            gb_send.at[d],
            gb_recv.at[d],
            at(g, rank),
        )

    for d in range(1, experts):
        from_line(d, line).start()
    gback[rows_at(line, srows), :] = brows[rows_at(line, srows), :]
    q_out.start()
    for d in range(1, experts):
        from_line(d, turn(line, -d)).wait_recv()
    zback[...] = jnp.dot(inverse, gback[...], preferred_element_type=F32).astype(BF16)

    b_out = Exchange(
        "exp",
        lambda t: zback.at[rows_at(t, zrows)],
        lambda s: bland.at[rows_at(s, zrows)],
        b_send,
        b_recv,
    )
    b_out.start()
    bland[rows_at(exp, zrows), :] = zback[rows_at(exp, zrows), :]
    q_own.wait()
    q_out.arrived()
    b_out.arrived()
    back_ref[...] = bland[...]
    for exchange in (z_out, q_out, b_out):
        exchange.sent()
    for d in range(1, experts):
        for each in weights:
            weight_copy(d, line, *each).wait_send()
        to_line(d, line).wait_send()
        from_line(d, line).wait_send()
    for d in range(experts):
        up(d, rank).wait_send()
        down(d, rank).wait_send()
        forwarded(d, rank).wait_send()
    for copy in (far_up, far_down, *near):
        copy.wait_send()


def attend_kernel(
    rows_ref,
    wk_ref,
    wv_ref,
    q_ref,
    out_ref,
    kvsend,
    kvland,
    csend,
    cland,
    k_send,
    k_recv,
    c_send,
    c_recv,
):
    seq = lax.axis_index("seq")
    n_seq = lax.axis_size("seq")
    count = rows_ref.shape[0]
    barrier, greeted = signal_all(("seq",))
    pl.semaphore_wait(barrier, greeted)
    lane = lax.broadcasted_iota(jnp.int32, (count, 128), 1)
    low = lane < 64
    block = rows_ref[...]
    for g in range(HEADS // 4):
        cols = slice(g * 256, (g + 1) * 256)
        keys = jnp.dot(block, wk_ref[:, cols], preferred_element_type=F32)
        values = jnp.dot(block, wv_ref[:, cols], preferred_element_type=F32)
        for i in range(2):
            k_pair = pltpu.roll(keys[:, i * 128 : (i + 1) * 128], 64, 1)
            v_pair = values[:, i * 128 : (i + 1) * 128]
            head = g * 4 + i * 2
            kvsend[head] = jnp.where(low, v_pair, k_pair).astype(BF16)
            kvsend[head + 1] = jnp.where(low, k_pair, v_pair).astype(BF16)
    kv_out = Exchange(
        "seq",
        lambda t: kvsend.at[t],
        lambda s: kvland.at[rows_at(s, count)],
        k_send,
        k_recv,
    )
    kv_out.start()
    kvland[rows_at(seq, count), :] = kvsend[seq]
    kv_out.arrived()

    c_out = Exchange("seq", lambda t: csend.at[t], lambda s: cland.at[s], c_send, c_recv)

    def attend(t):
        kv = kvland[...]
        scores = lax.dot_general(
            q_ref[t], kv, (((1,), (1,)), ((), ())), preferred_element_type=F32
        )
        expo = jnp.exp(scores - jnp.max(scores, axis=-1, keepdims=True))
        total = jnp.sum(expo, axis=-1, keepdims=True)
        mixed = jnp.dot(expo.astype(BF16), kv, preferred_element_type=F32)
        return (mixed / total).astype(BF16)

    def step(d, carry):
        t = lax.rem(seq + d, n_seq)
        csend[t] = attend(t)
        c_out.start_one(d)
        return carry

    lax.fori_loop(1, n_seq, step, 0)
    cland[seq] = attend(seq)
    c_out.arrived()
    low = lax.broadcasted_iota(jnp.int32, cland.shape[1:], 1) < 64
    for p in range(HEADS // 2):
        out_ref[:, p * 128 : (p + 1) * 128] = jnp.where(low, cland[2 * p], cland[2 * p + 1])
    kv_out.sent()
    c_out.sent()


def per_device(
    enc_in,
    expert_ids,
    slots,
    expert_gate,
    moe_gain,
    w_in,
    w_out,
    final_gain,
    w_key,
    w_value,
    dec_query,
):
    n_exp, n_seq = lax.axis_size("exp"), lax.axis_size("seq")
    tok_rows, width = enc_in.shape[1:]
    experts, _, part_ff = w_in.shape
    capacity = tok_rows // (experts * n_exp)
    q_rows = dec_query.shape[1]

    vmem = pl.BlockSpec(memory_space=pltpu.VMEM)
    hbm = pl.BlockSpec(memory_space=pl.ANY)
    dma = pltpu.SemaphoreType.DMA
    whole = pltpu.VMEM((tok_rows, width), BF16)
    half = pltpu.VMEM((tok_rows // 2, width), F32)
    full = pltpu.VMEM((tok_rows, width), F32)
    weight = pltpu.VMEM((experts * part_ff, width), BF16)
    back, queries = pl.pallas_call(
        moe_kernel,
        out_shape=(
            jax.ShapeDtypeStruct((tok_rows, width), BF16),
            jax.ShapeDtypeStruct((n_seq, q_rows, 128), BF16),
        ),
        in_specs=[hbm, vmem, vmem, vmem, hbm, hbm, hbm],
        out_specs=(vmem, hbm),
        scratch_shapes=[
            whole,
            pltpu.VMEM((q_rows, width), BF16),
            whole,
            whole,
            whole,
            pltpu.VMEM((experts, tok_rows, width), BF16),
            weight,
            weight,
            pltpu.VMEM((experts, tok_rows, width), F32),
            half,
            half,
            full,
            full,
            whole,
            whole,
            whole,
            whole,
            pltpu.VMEM((n_seq, q_rows, 128), BF16),
            dma((4,)),
        ]
        + [dma((n_exp,))] * 4
        + [dma((n_seq,))] * 2
        + [dma((experts,))] * 12
        + [dma((2,))] * 2
        + [dma((4,))] * 2
        + [dma((experts,))] * 2,
        compiler_params=pltpu.CompilerParams(
            collective_id=0, has_side_effects=True, vmem_limit_bytes=56 << 20
        ),
        name="experts",
    )(
        enc_in[0],
        expert_ids,
        slots,
        moe_gain[None],
        jnp.swapaxes(w_in, 1, 2),
        w_out,
        dec_query[0],
    )

    inputs = enc_in[0].astype(F32)
    places = jnp.arange(tok_rows, dtype=jnp.int32)
    target = jnp.where(slots[0] < capacity, expert_ids[0] * capacity + slots[0], -1)
    combine = (target[:, None] == places[None, :]).astype(BF16)
    combined = jnp.dot(combine, back, preferred_element_type=F32)
    enc_rows = inputs + expert_gate[0][:, None] * combined
    enc_out = enc_rows.astype(BF16)
    kv_rows = rms_scale(enc_out.astype(F32), final_gain).astype(BF16)
    context = pl.pallas_call(
        attend_kernel,
        out_shape=jax.ShapeDtypeStruct((q_rows, width), BF16),
        in_specs=[vmem] * 4,
        out_specs=vmem,
        scratch_shapes=[
            pltpu.VMEM((n_seq, tok_rows, 128), BF16),
            pltpu.VMEM((n_seq * tok_rows, 128), BF16),
            pltpu.VMEM((n_seq, q_rows, 128), BF16),
            pltpu.VMEM((n_seq, q_rows, 128), BF16),
        ]
        + [dma((n_seq,))] * 4,
        compiler_params=pltpu.CompilerParams(
            collective_id=1, has_side_effects=True, vmem_limit_bytes=40 << 20
        ),
        name="attend",
    )(kv_rows, w_key, w_value, queries)
    return (enc_out[None], context[None])


def solution(mesh):
    placed = (
        P("exp", "seq", None),
        P("exp", "seq"),
        P("exp", "seq"),
        P("exp", "seq"),
        P(),
        P("exp", None, "seq"),
        P("exp", "seq", None),
        P(),
        P(),
        P(),
        P("exp", "seq", None),
    )
    return jax.shard_map(
        per_device,
        mesh=mesh,
        in_specs=placed,
        out_specs=(P("exp", "seq", None), P("exp", "seq", None)),
        check_vma=False,
    )
```

```python
import functools

import jax
import jax.numpy as jnp
from jax import lax
from jax.experimental import pallas as pl
from jax.experimental.pallas import tpu as pltpu
from jax.sharding import PartitionSpec as P

HEADS = 16
CHUNKS = 2
MESH = pl.DeviceIdType.MESH
F32 = jnp.float32
BF16 = jnp.bfloat16


def rms_scale(values, gain):
    mean_square = jnp.mean(values * values, axis=-1, keepdims=True)
    return values * lax.rsqrt(mean_square + 1e-06) * gain


def rows_at(index, count):
    return pl.ds(pl.multiple_of(index * count, count), count)


def signal_all(axes):
    barrier = pltpu.get_barrier_semaphore()
    total = 0
    for axis in axes:
        n = lax.axis_size(axis)
        me = lax.axis_index(axis)
        total += n - 1

        def signal(d, carry, axis=axis, n=n, me=me):
            pl.semaphore_signal(
                barrier, inc=1, device_id={axis: lax.rem(me + d, n)}, device_id_type=MESH
            )
            return carry

        lax.fori_loop(1, n, signal, 0)
    return barrier, total


class Exchange:
    def __init__(self, axis, source, landing, send, recv):
        self.axis, self.source, self.landing = axis, source, landing
        self.send, self.recv = send, recv
        self.n, self.me = lax.axis_size(axis), lax.axis_index(axis)

    def copy(self, d, slot):
        t = lax.rem(self.me + d, self.n)
        return pltpu.make_async_remote_copy(
            src_ref=self.source(t),
            dst_ref=self.landing(slot),
            send_sem=self.send.at[d],
            recv_sem=self.recv.at[d],
            device_id={self.axis: t},
            device_id_type=MESH,
        )

    def start_one(self, d):
        self.copy(d, self.me).start()

    def wait_one(self, d):
        self.copy(d, lax.rem(self.me + self.n - d, self.n)).wait_recv()

    def loop(self, act):
        def body(d, carry):
            act(d)
            return carry

        lax.fori_loop(1, self.n, body, 0)

    def start(self):
        self.loop(self.start_one)

    def arrived(self):
        self.loop(self.wait_one)

    def sent(self):
        self.loop(lambda d: self.copy(d, self.me).wait_send())


def remote(src, dst, send, recv, seq):
    return pltpu.make_async_remote_copy(
        src_ref=src,
        dst_ref=dst,
        send_sem=send,
        recv_sem=recv,
        device_id={"seq": seq},
        device_id_type=MESH,
    )


def moe_kernel(
    enc_ref,
    ids_ref,
    slots_ref,
    gain_ref,
    win_ref,
    wout_ref,
    q_ref,
    back_ref,
    qland_ref,
    enc,
    query,
    packed,
    zland,
    rows,
    rland,
    win_land,
    wout_land,
    relay,
    hidden,
    part,
    half_up,
    half_down,
    full_up,
    full_down,
    brows,
    gback,
    zback,
    bland,
    qsend,
    local_sem,
    z_send,
    z_recv,
    b_send,
    b_recv,
    q_send,
    q_recv,
    wi_send,
    wi_recv,
    wo_send,
    wo_recv,
    relay_send,
    relay_recv,
    g_send,
    g_recv,
    up_send,
    up_recv,
    down_send,
    down_recv,
    fwd_send,
    fwd_recv,
    h_send,
    h_recv,
    f_send,
    f_recv,
    gb_send,
    gb_recv,
):
    seq, exp = lax.axis_index("seq"), lax.axis_index("exp")
    n_seq, n_exp = lax.axis_size("seq"), lax.axis_size("exp")
    experts = win_ref.shape[0]
    hidden_part = win_ref.shape[1]
    tok = enc_ref.shape[0]
    zrows, srows = tok // n_exp, tok // experts
    capacity = zrows // experts
    core = lax.rem(exp, 2)
    y, x = seq // experts, lax.rem(seq, experts)
    line, rank = y + core * (x - y), x + core * (y - x)

    def at(g, r):
        return g * (experts - core * (experts - 1)) + r * (1 + core * (experts - 1))

    def turn(value, d):
        return lax.rem(value + experts + d, experts)

    enc_in = pltpu.make_async_copy(enc_ref, enc, local_sem.at[0])
    q_in = pltpu.make_async_copy(q_ref, query, local_sem.at[1])
    enc_in.start()
    q_in.start()
    barrier, greeted = signal_all(("seq", "exp"))
    own_weights = [
        pltpu.make_async_copy(
            ref.at[line], land.at[rows_at(line, hidden_part)], local_sem.at[2 + i]
        )
        for i, (ref, land) in enumerate(((win_ref, win_land), (wout_ref, wout_land)))
    ]
    for copy in own_weights:
        copy.start()
    enc_in.wait()
    normed = rms_scale(enc[...].astype(F32), gain_ref[...]).astype(BF16)
    target = jnp.where(slots_ref[...] < capacity, ids_ref[...] * capacity + slots_ref[...], -1)
    out_row = lax.broadcasted_iota(jnp.int32, (tok, tok), 0)
    in_row = lax.broadcasted_iota(jnp.int32, (tok, tok), 1)
    dispatch = (out_row == target).astype(BF16)
    packed[...] = jnp.dot(dispatch, normed, preferred_element_type=F32).astype(BF16)
    pl.semaphore_wait(barrier, greeted)

    chunks = z_send.shape[0]
    wide = enc_ref.shape[1] // chunks

    def cols(c):
        return pl.ds(c * wide, wide)

    def z_out(c):
        return Exchange(
            "exp",
            lambda t: packed.at[rows_at(t, zrows), cols(c)],
            lambda s: zland.at[rows_at(s, zrows), cols(c)],
            z_send.at[c],
            z_recv.at[c],
        )

    def weight_copy(d, slot, ref, land, send, recv):
        k = turn(line, d)
        return remote(
            ref.at[k], land.at[rows_at(slot, hidden_part)], send.at[d], recv.at[d], at(k, rank)
        )

    relay_in = remote(
        wout_ref.at[turn(line, 2)],
        relay,
        relay_send.at[0],
        relay_recv.at[0],
        at(turn(line, -1), rank),
    )

    def relay_out(slot):
        return remote(
            relay,
            wout_land.at[rows_at(slot, hidden_part)],
            relay_send.at[1],
            relay_recv.at[1],
            at(turn(line, -1), rank),
        )

    w_first = (win_ref, win_land, wi_send, wi_recv)
    w_second = (wout_ref, wout_land, wo_send, wo_recv)
    direct = [(d, w_first) for d in range(1, experts)] + [(d, w_second) for d in (1, 3)]
    z_out(0).start()
    relay_in.start()
    for d, each in direct:
        weight_copy(d, line, *each).start()
    for c in range(1, chunks):
        z_out(c).start()
    zland[rows_at(exp, zrows), :] = packed[rows_at(exp, zrows), :]

    q_in.wait()
    lane = lax.broadcasted_iota(jnp.int32, (q_ref.shape[0], 128), 1)
    for p in range(HEADS // 2):
        pair = pltpu.roll(query[:, p * 128 : (p + 1) * 128].astype(F32) * 0.125, 64, 1)
        qsend[2 * p] = jnp.where(lane >= 64, pair, 0.0).astype(BF16)
        qsend[2 * p + 1] = jnp.where(lane < 64, pair, 0.0).astype(BF16)
    q_out = Exchange(
        "seq", lambda t: qsend.at[t], lambda s: qland_ref.at[s], q_send, q_recv
    )
    q_own = pltpu.make_async_copy(qsend.at[seq], qland_ref.at[seq], local_sem.at[0])
    q_own.start()

    def by_expert(r):
        j, k, c = r // zrows, lax.rem(r // capacity, experts), lax.rem(r, capacity)
        return k * srows + j * capacity + c

    forward = (by_expert(in_row) == out_row).astype(BF16)
    inverse = (by_expert(out_row) == in_row).astype(BF16)
    relay_in.wait_recv()
    relay_out(turn(line, 1)).start()

    above, below, across = turn(rank, 1), turn(rank, -1), turn(rank, 2)

    def piece(r, g, c):
        return rland.at[r, rows_at(g, srows), cols(c)]

    def to_line(c, d, slot):
        k = turn(line, d)
        return remote(
            rows.at[rows_at(k, srows), cols(c)],
            piece(rank, slot, c),
            g_send.at[c, d],
            g_recv.at[c, d],
            at(k, rank),
        )

    def up(c, d, r):
        g = turn(line, -d)
        return remote(
            piece(rank, g, c), piece(r, g, c), up_send.at[c, d], up_recv.at[c, d], at(line, above)
        )

    def down(c, d, r):
        g = turn(line, -d)
        return remote(
            piece(rank, g, c),
            piece(r, g, c),
            down_send.at[c, d],
            down_recv.at[c, d],
            at(line, below),
        )

    def forwarded(c, d, r):
        g = turn(line, -d)
        way = 1 if d < 2 else -1
        return remote(
            piece(turn(rank, -way), g, c),
            piece(r, g, c),
            fwd_send.at[c, d],
            fwd_recv.at[c, d],
            at(line, turn(rank, way)),
        )

    for c in range(chunks):
        z_out(c).arrived()
        rows[:, cols(c)] = jnp.dot(
            forward, zland[:, cols(c)], preferred_element_type=F32
        ).astype(BF16)
        for d in range(1, experts):
            to_line(c, d, line).start()
        rland[rank, rows_at(line, srows), cols(c)] = rows[rows_at(line, srows), cols(c)]
        for d in range(experts):
            if d:
                to_line(c, d, turn(line, -d)).wait_recv()
            up(c, d, rank).start()
            down(c, d, rank).start()
        for d in (0, 1):
            up(c, d, below).wait_recv()
            forwarded(c, d, below).start()
        for d in (2, 3):
            down(c, d, above).wait_recv()
            forwarded(c, d, above).start()

    def first_layer(r):
        product = lax.dot_general(
            rland[r], win_land[...], (((1,), (1,)), ((), ())), preferred_element_type=F32
        )
        hidden[r] = jnp.maximum(product, 0.0).astype(BF16)

    for copy in own_weights:
        copy.wait()
    for d, each in direct:
        if each is w_first:
            weight_copy(d, turn(line, -d), *each).wait_recv()
    first_layer(rank)
    for c in range(chunks):
        for d in (2, 3):
            up(c, d, below).wait_recv()
    first_layer(below)
    for c in range(chunks):
        for d in (0, 1):
            down(c, d, above).wait_recv()
    first_layer(above)
    for c in range(chunks):
        for d in range(experts):
            forwarded(c, d, across).wait_recv()
    first_layer(across)
    for d, each in direct:
        if each is w_second:
            weight_copy(d, turn(line, -d), *each).wait_recv()
    relay_out(turn(line, 2)).wait_recv()

    mid = tok // 2
    first, second = pl.ds(0, mid), pl.ds(mid, mid)

    def far(c, way):
        half, land, r = ((first, half_up, above), (second, half_down, below))[way]
        return remote(
            part.at[across, half, cols(c)],
            land.at[:, cols(c)],
            h_send.at[c, way],
            h_recv.at[c, way],
            at(line, r),
        )

    def near(c, i):
        r, half, land = (
            (above, second, full_up),
            (below, first, full_down),
            (above, first, full_up),
            (below, second, full_down),
        )[i]
        return remote(
            part.at[r, half, cols(c)],
            land.at[half, cols(c)],
            f_send.at[c, i],
            f_recv.at[c, i],
            at(line, r),
        )

    def from_line(c, d, slot):
        g = turn(line, d)
        return remote(
            brows.at[rows_at(g, srows), cols(c)],
            gback.at[rows_at(slot, srows), cols(c)],
            gb_send.at[c, d],
            gb_recv.at[c, d],
            at(g, rank),
        )

    def b_out(c):
        return Exchange(
            "exp",
            lambda t: zback.at[rows_at(t, zrows), cols(c)],
            lambda s: bland.at[rows_at(s, zrows), cols(c)],
            b_send.at[c],
            b_recv.at[c],
        )

    def second_layer(c):
        def one(r):
            part[r, :, cols(c)] = jnp.dot(
                hidden[r], wout_land[:, cols(c)], preferred_element_type=F32
            )

        one(across)
        far(c, 0).start()
        far(c, 1).start()
        one(above)
        near(c, 0).start()
        one(below)
        near(c, 1).start()
        one(rank)

    def add_far(c):
        far(c, 0).wait_recv()
        part[above, first, cols(c)] = part[above, first, cols(c)] + half_up[:, cols(c)]
        near(c, 2).start()
        far(c, 1).wait_recv()
        part[below, second, cols(c)] = part[below, second, cols(c)] + half_down[:, cols(c)]
        near(c, 3).start()

    def finish(c):
        for i in (0, 1, 2, 3):
            near(c, i).wait_recv()
        brows[:, cols(c)] = (
            part[rank, :, cols(c)] + full_up[:, cols(c)] + full_down[:, cols(c)]
        ).astype(BF16)
        for d in range(1, experts):
            from_line(c, d, line).start()
        gback[rows_at(line, srows), cols(c)] = brows[rows_at(line, srows), cols(c)]

    def give_back(c):
        for d in range(1, experts):
            from_line(c, d, turn(line, -d)).wait_recv()
        zback[:, cols(c)] = jnp.dot(
            inverse, gback[:, cols(c)], preferred_element_type=F32
        ).astype(BF16)
        b_out(c).start()
        bland[rows_at(exp, zrows), cols(c)] = zback[rows_at(exp, zrows), cols(c)]

    second_layer(0)
    add_far(0)
    for c in range(1, chunks):
        second_layer(c)
        finish(c - 1)
        add_far(c)
        give_back(c - 1)
    finish(chunks - 1)
    q_out.start()
    give_back(chunks - 1)

    q_own.wait()
    q_out.arrived()
    for c in range(chunks):
        b_out(c).arrived()
    back_ref[...] = bland[...]
    q_out.sent()
    for d, each in direct:
        weight_copy(d, line, *each).wait_send()
    relay_in.wait_send()
    relay_out(line).wait_send()
    for c in range(chunks):
        z_out(c).sent()
        b_out(c).sent()
        for d in range(experts):
            if d:
                to_line(c, d, line).wait_send()
                from_line(c, d, line).wait_send()
            up(c, d, rank).wait_send()
            down(c, d, rank).wait_send()
            forwarded(c, d, rank).wait_send()
        for i in range(4):
            near(c, i).wait_send()
        for way in range(2):
            far(c, way).wait_send()


def attend_kernel(
    rows_ref,
    wk_ref,
    wv_ref,
    q_ref,
    out_ref,
    kvsend,
    kvland,
    vland,
    qrows,
    csend,
    cland,
    k_send,
    k_recv,
    c_send,
    c_recv,
):
    seq = lax.axis_index("seq")
    n_seq = lax.axis_size("seq")
    count = rows_ref.shape[0]
    barrier, greeted = signal_all(("seq",))
    pl.semaphore_wait(barrier, greeted)
    lane = lax.broadcasted_iota(jnp.int32, (count, 128), 1)
    low = lane < 64
    block = rows_ref[...]
    for g in range(HEADS // 4):
        cols = slice(g * 256, (g + 1) * 256)
        keys = jnp.dot(block, wk_ref[:, cols], preferred_element_type=F32)
        values = jnp.dot(block, wv_ref[:, cols], preferred_element_type=F32)
        for i in range(2):
            k_pair = pltpu.roll(keys[:, i * 128 : (i + 1) * 128], 64, 1)
            v_pair = values[:, i * 128 : (i + 1) * 128]
            head = g * 4 + i * 2
            kvsend[head] = jnp.where(low, v_pair, k_pair).astype(BF16)
            kvsend[head + 1] = jnp.where(low, k_pair, v_pair).astype(BF16)
    kv_out = Exchange(
        "seq",
        lambda t: kvsend.at[t],
        lambda s: kvland.at[rows_at(s, count)],
        k_send,
        k_recv,
    )
    kv_out.start()
    kvland[rows_at(seq, count), :] = kvsend[seq]
    kv_out.arrived()

    c_out = Exchange("seq", lambda t: csend.at[rows_at(t, q_ref.shape[1])], lambda s: cland.at[s], c_send, c_recv)

    wide_lane = lax.broadcasted_iota(jnp.int32, kvland.shape, 1)
    key_side = 64 * (1 - lax.rem(seq, 2))
    is_key = (wide_lane >= key_side) & (wide_lane < key_side + 64)
    vland[...] = jnp.where(is_key, jnp.ones((), BF16), kvland[...])
    pair_rows = 2 * q_ref.shape[1]

    def scores_of(i):
        return lax.dot_general(
            qrows[rows_at(i, pair_rows), :],
            kvland[...],
            (((1,), (1,)), ((), ())),
            preferred_element_type=F32,
        )

    def context_of(scores):
        expo = jnp.exp(scores - jnp.max(scores, axis=-1, keepdims=True))
        mixed = jnp.dot(expo.astype(BF16), vland[...], preferred_element_type=F32)
        return (mixed / pltpu.roll(mixed, 64, 1)).astype(BF16)

    qrows[...] = q_ref[...].reshape(qrows.shape)
    group = 4

    def step(d, carry):
        g = lax.rem(seq // group + d, n_seq // group)
        both = [scores_of(2 * g + i) for i in range(2)]
        for i in range(2):
            csend[rows_at(2 * g + i, pair_rows), :] = context_of(both[i])
        for i in range(group):
            t = g * group + i

            @pl.when(t != seq)
            def _():
                c_out.start_one(lax.rem(t - seq + n_seq, n_seq))

        return carry

    lax.fori_loop(0, n_seq // group, step, 0)
    cland[seq] = csend[rows_at(seq, q_ref.shape[1]), :]
    c_out.arrived()
    low = lax.broadcasted_iota(jnp.int32, cland.shape[1:], 1) < 64
    for p in range(HEADS // 2):
        out_ref[:, p * 128 : (p + 1) * 128] = jnp.where(low, cland[2 * p], cland[2 * p + 1])
    kv_out.sent()
    c_out.sent()


def per_device(
    enc_in,
    expert_ids,
    slots,
    expert_gate,
    moe_gain,
    w_in,
    w_out,
    final_gain,
    w_key,
    w_value,
    dec_query,
):
    n_exp, n_seq = lax.axis_size("exp"), lax.axis_size("seq")
    tok_rows, width = enc_in.shape[1:]
    experts, _, part_ff = w_in.shape
    capacity = tok_rows // (experts * n_exp)
    q_rows = dec_query.shape[1]

    vmem = pl.BlockSpec(memory_space=pltpu.VMEM)
    hbm = pl.BlockSpec(memory_space=pl.ANY)
    dma = pltpu.SemaphoreType.DMA
    whole = pltpu.VMEM((tok_rows, width), BF16)
    half = pltpu.VMEM((tok_rows // 2, width), F32)
    full = pltpu.VMEM((tok_rows, width), F32)
    weight = pltpu.VMEM((experts * part_ff, width), BF16)
    back, queries = pl.pallas_call(
        moe_kernel,
        out_shape=(
            jax.ShapeDtypeStruct((tok_rows, width), BF16),
            jax.ShapeDtypeStruct((n_seq, q_rows, 128), BF16),
        ),
        in_specs=[hbm, vmem, vmem, vmem, hbm, hbm, hbm],
        out_specs=(vmem, hbm),
        scratch_shapes=[
            whole,
            pltpu.VMEM((q_rows, width), BF16),
            whole,
            whole,
            whole,
            pltpu.VMEM((experts, tok_rows, width), BF16),
            weight,
            weight,
            pltpu.VMEM((part_ff, width), BF16),
            pltpu.VMEM((experts, tok_rows, experts * part_ff), BF16),
            pltpu.VMEM((experts, tok_rows, width), F32),
            half,
            half,
            full,
            full,
            whole,
            whole,
            whole,
            whole,
            pltpu.VMEM((n_seq, q_rows, 128), BF16),
            dma((4,)),
        ]
        + [dma((CHUNKS, n_exp))] * 4
        + [dma((n_seq,))] * 2
        + [dma((experts,))] * 4
        + [dma((2,))] * 2
        + [dma((CHUNKS, experts))] * 8
        + [dma((CHUNKS, 2))] * 2
        + [dma((CHUNKS, 4))] * 2
        + [dma((CHUNKS, experts))] * 2,
        compiler_params=pltpu.CompilerParams(
            collective_id=0, has_side_effects=True, vmem_limit_bytes=56 << 20
        ),
        name="experts",
    )(
        enc_in[0],
        expert_ids,
        slots,
        moe_gain[None],
        jnp.swapaxes(w_in, 1, 2),
        w_out,
        dec_query[0],
    )

    inputs = enc_in[0].astype(F32)
    places = jnp.arange(tok_rows, dtype=jnp.int32)
    target = jnp.where(slots[0] < capacity, expert_ids[0] * capacity + slots[0], -1)
    combine = (target[:, None] == places[None, :]).astype(BF16)
    combined = jnp.dot(combine, back, preferred_element_type=F32)
    enc_rows = inputs + expert_gate[0][:, None] * combined
    enc_out = enc_rows.astype(BF16)
    kv_rows = rms_scale(enc_out.astype(F32), final_gain).astype(BF16)
    context = pl.pallas_call(
        attend_kernel,
        out_shape=jax.ShapeDtypeStruct((q_rows, width), BF16),
        in_specs=[vmem] * 4,
        out_specs=vmem,
        scratch_shapes=[
            pltpu.VMEM((n_seq, tok_rows, 128), BF16),
            pltpu.VMEM((n_seq * tok_rows, 128), BF16),
            pltpu.VMEM((n_seq * tok_rows, 128), BF16),
            pltpu.VMEM((n_seq * q_rows, 128), BF16),
            pltpu.VMEM((n_seq * q_rows, 128), BF16),
            pltpu.VMEM((n_seq, q_rows, 128), BF16),
        ]
        + [dma((n_seq,))] * 4,
        compiler_params=pltpu.CompilerParams(
            collective_id=1, has_side_effects=True, vmem_limit_bytes=40 << 20
        ),
        name="attend",
    )(kv_rows, w_key, w_value, queries)
    return (enc_out[None], context[None])


def solution(mesh):
    placed = (
        P("exp", "seq", None),
        P("exp", "seq"),
        P("exp", "seq"),
        P("exp", "seq"),
        P(),
        P("exp", None, "seq"),
        P("exp", "seq", None),
        P(),
        P(),
        P(),
        P("exp", "seq", None),
    )
    return jax.shard_map(
        per_device,
        mesh=mesh,
        in_specs=placed,
        out_specs=(P("exp", "seq", None), P("exp", "seq", None)),
        check_vma=False,
    )
```

```python
import functools

import jax
import jax.numpy as jnp
from jax import lax
from jax.experimental import pallas as pl
from jax.experimental.pallas import tpu as pltpu
from jax.sharding import PartitionSpec as P

HEADS = 16
OUT_CHUNKS = 1
BACK_CHUNKS = 2
MESH = pl.DeviceIdType.MESH
F32 = jnp.float32
BF16 = jnp.bfloat16


def rms_scale(values, gain):
    mean_square = jnp.mean(values * values, axis=-1, keepdims=True)
    return values * lax.rsqrt(mean_square + 1e-06) * gain


def rows_at(index, count):
    return pl.ds(pl.multiple_of(index * count, count), count)


def signal_all(axes):
    barrier = pltpu.get_barrier_semaphore()
    total = 0
    for axis in axes:
        n = lax.axis_size(axis)
        me = lax.axis_index(axis)
        total += n - 1

        def signal(d, carry, axis=axis, n=n, me=me):
            pl.semaphore_signal(
                barrier, inc=1, device_id={axis: lax.rem(me + d, n)}, device_id_type=MESH
            )
            return carry

        lax.fori_loop(1, n, signal, 0)
    return barrier, total


class Exchange:
    def __init__(self, axis, source, landing, send, recv):
        self.axis, self.source, self.landing = axis, source, landing
        self.send, self.recv = send, recv
        self.n, self.me = lax.axis_size(axis), lax.axis_index(axis)

    def copy(self, d, slot):
        t = lax.rem(self.me + d, self.n)
        return pltpu.make_async_remote_copy(
            src_ref=self.source(t),
            dst_ref=self.landing(slot),
            send_sem=self.send.at[d],
            recv_sem=self.recv.at[d],
            device_id={self.axis: t},
            device_id_type=MESH,
        )

    def start_one(self, d):
        self.copy(d, self.me).start()

    def wait_one(self, d):
        self.copy(d, lax.rem(self.me + self.n - d, self.n)).wait_recv()

    def loop(self, act):
        def body(d, carry):
            act(d)
            return carry

        lax.fori_loop(1, self.n, body, 0)

    def start(self):
        self.loop(self.start_one)

    def arrived(self):
        self.loop(self.wait_one)

    def wait_send(self):
        self.loop(lambda d: self.copy(d, self.me).wait_send())


def remote(src, dst, send, recv, seq):
    return pltpu.make_async_remote_copy(
        src_ref=src,
        dst_ref=dst,
        send_sem=send,
        recv_sem=recv,
        device_id={"seq": seq},
        device_id_type=MESH,
    )


def moe_kernel(
    enc_ref,
    ids_ref,
    slots_ref,
    gain_ref,
    win_ref,
    wout_ref,
    q_ref,
    back_ref,
    qland_ref,
    enc,
    query,
    packed,
    zland,
    rows,
    rland,
    win_land,
    wout_land,
    relay,
    hidden,
    far_part,
    up_part,
    down_part,
    up_wait,
    down_wait,
    own_part,
    half_up,
    half_down,
    full_up,
    full_down,
    brows,
    gback,
    zback,
    bland,
    qsend,
    local_sem,
    z_send,
    z_recv,
    b_send,
    b_recv,
    q_send,
    q_recv,
    wi_send,
    wi_recv,
    wo_send,
    wo_recv,
    relay_send,
    relay_recv,
    g_send,
    g_recv,
    up_send,
    up_recv,
    down_send,
    down_recv,
    fwd_send,
    fwd_recv,
    h_send,
    h_recv,
    f_send,
    f_recv,
    gb_send,
    gb_recv,
):
    seq, exp = lax.axis_index("seq"), lax.axis_index("exp")
    n_seq, n_exp = lax.axis_size("seq"), lax.axis_size("exp")
    experts = win_ref.shape[0]
    hidden_part = win_ref.shape[1]
    tok = enc_ref.shape[0]
    zrows, srows = tok // n_exp, tok // experts
    capacity = zrows // experts
    core = lax.rem(exp, 2)
    y, x = seq // experts, lax.rem(seq, experts)
    line, rank = y + core * (x - y), x + core * (y - x)

    def at(g, r):
        return g * (experts - core * (experts - 1)) + r * (1 + core * (experts - 1))

    def turn(value, d):
        return lax.rem(value + experts + d, experts)

    enc_in = pltpu.make_async_copy(enc_ref, enc, local_sem.at[0])
    q_in = pltpu.make_async_copy(q_ref, query, local_sem.at[1])
    enc_in.start()
    q_in.start()
    barrier, greeted = signal_all(("seq", "exp"))
    own_weights = [
        pltpu.make_async_copy(
            ref.at[line], land.at[rows_at(line, hidden_part)], local_sem.at[2 + i]
        )
        for i, (ref, land) in enumerate(((win_ref, win_land), (wout_ref, wout_land)))
    ]
    for copy in own_weights:
        copy.start()
    enc_in.wait()
    normed = rms_scale(enc[...].astype(F32), gain_ref[...]).astype(BF16)
    target = jnp.where(slots_ref[...] < capacity, ids_ref[...] * capacity + slots_ref[...], -1)
    out_row = lax.broadcasted_iota(jnp.int32, (tok, tok), 0)
    in_row = lax.broadcasted_iota(jnp.int32, (tok, tok), 1)
    dispatch = (out_row == target).astype(BF16)
    packed[...] = jnp.dot(dispatch, normed, preferred_element_type=F32).astype(BF16)
    q_in.wait()
    q_half = q_ref.shape[0] // 2
    lane = lax.broadcasted_iota(jnp.int32, (q_half, 128), 1)
    for p in range(HEADS // 2):
        pair = query[:, p * 128 : (p + 1) * 128].astype(F32) * 0.125
        turned = pltpu.roll(pair, 64, 1)
        qsend[2 * p] = jnp.where(lane < 64, pair[:q_half], turned[q_half:]).astype(BF16)
        qsend[2 * p + 1] = jnp.where(lane < 64, turned[:q_half], pair[q_half:]).astype(BF16)
    pl.semaphore_wait(barrier, greeted)

    started = []

    def go(transfer):
        transfer.start()
        started.append(transfer)

    chunks, back_chunks = z_send.shape[0], b_send.shape[0]
    wide = enc_ref.shape[1] // chunks
    back_wide = enc_ref.shape[1] // back_chunks

    def cols(c):
        return pl.ds(c * wide, wide)

    def bcols(c):
        return pl.ds(c * back_wide, back_wide)

    def z_out(c):
        return Exchange(
            "exp",
            lambda t: packed.at[rows_at(t, zrows), cols(c)],
            lambda s: zland.at[rows_at(s, zrows), cols(c)],
            z_send.at[c],
            z_recv.at[c],
        )

    def weight_copy(d, slot, ref, land, send, recv):
        k = turn(line, d)
        return remote(
            ref.at[k], land.at[rows_at(slot, hidden_part)], send.at[d], recv.at[d], at(k, rank)
        )

    relay_in = remote(
        wout_ref.at[turn(line, 2)],
        relay,
        relay_send.at[0],
        relay_recv.at[0],
        at(turn(line, -1), rank),
    )

    def relay_out(slot):
        return remote(
            relay,
            wout_land.at[rows_at(slot, hidden_part)],
            relay_send.at[1],
            relay_recv.at[1],
            at(turn(line, -1), rank),
        )

    w_first = (win_ref, win_land, wi_send, wi_recv)
    w_second = (wout_ref, wout_land, wo_send, wo_recv)
    direct = [(d, w_first) for d in range(1, experts)] + [(d, w_second) for d in (1, 3)]
    go(z_out(0))
    q_out = Exchange(
        "seq", lambda t: qsend.at[t], lambda s: qland_ref.at[s], q_send, q_recv
    )
    q_own = pltpu.make_async_copy(qsend.at[seq], qland_ref.at[seq], local_sem.at[0])
    q_own.start()
    go(q_out)
    go(relay_in)
    for d, each in direct:
        go(weight_copy(d, line, *each))
    for c in range(1, chunks):
        go(z_out(c))
    zland[rows_at(exp, zrows), :] = packed[rows_at(exp, zrows), :]

    def by_expert(r):
        j, k, c = r // zrows, lax.rem(r // capacity, experts), lax.rem(r, capacity)
        return k * srows + j * capacity + c

    forward = (by_expert(in_row) == out_row).astype(BF16)
    inverse = (by_expert(out_row) == in_row).astype(BF16)
    relay_in.wait_recv()
    go(relay_out(turn(line, 1)))

    above, below, across = turn(rank, 1), turn(rank, -1), turn(rank, 2)

    def piece(r, g, c):
        return rland.at[r, rows_at(g, srows), cols(c)]

    def to_line(c, d, slot):
        k = turn(line, d)
        return remote(
            rows.at[rows_at(k, srows), cols(c)],
            piece(rank, slot, c),
            g_send.at[c, d],
            g_recv.at[c, d],
            at(k, rank),
        )

    def up(c, d, r):
        g = turn(line, -d)
        return remote(
            piece(rank, g, c), piece(r, g, c), up_send.at[c, d], up_recv.at[c, d], at(line, above)
        )

    def down(c, d, r):
        g = turn(line, -d)
        return remote(
            piece(rank, g, c),
            piece(r, g, c),
            down_send.at[c, d],
            down_recv.at[c, d],
            at(line, below),
        )

    def forwarded(c, d, r):
        g = turn(line, -d)
        way = 1 if d < 2 else -1
        return remote(
            piece(turn(rank, -way), g, c),
            piece(r, g, c),
            fwd_send.at[c, d],
            fwd_recv.at[c, d],
            at(line, turn(rank, way)),
        )

    for c in range(chunks):
        z_out(c).arrived()
        rows[:, cols(c)] = jnp.dot(
            forward, zland[:, cols(c)], preferred_element_type=F32
        ).astype(BF16)
        for d in range(1, experts):
            go(to_line(c, d, line))
        rland[rank, rows_at(line, srows), cols(c)] = rows[rows_at(line, srows), cols(c)]
        for d in range(experts):
            if d:
                to_line(c, d, turn(line, -d)).wait_recv()
            go(up(c, d, rank))
            go(down(c, d, rank))
        for d in (0, 1):
            up(c, d, below).wait_recv()
            go(forwarded(c, d, below))
        for d in (2, 3):
            down(c, d, above).wait_recv()
            go(forwarded(c, d, above))

    def first_layer(r):
        product = lax.dot_general(
            rland[r], win_land[...], (((1,), (1,)), ((), ())), preferred_element_type=F32
        )
        hidden[r] = jnp.maximum(product, 0.0).astype(BF16)

    for copy in own_weights:
        copy.wait()
    for d, each in direct:
        if each is w_first:
            weight_copy(d, turn(line, -d), *each).wait_recv()
    first_layer(rank)
    for c in range(chunks):
        for d in (2, 3):
            up(c, d, below).wait_recv()
    first_layer(below)
    for c in range(chunks):
        for d in (0, 1):
            down(c, d, above).wait_recv()
    first_layer(above)
    for c in range(chunks):
        for d in range(experts):
            forwarded(c, d, across).wait_recv()
    first_layer(across)
    for d, each in direct:
        if each is w_second:
            weight_copy(d, turn(line, -d), *each).wait_recv()
    relay_out(turn(line, 2)).wait_recv()

    mid = tok // 2
    first, second = pl.ds(0, mid), pl.ds(mid, mid)

    def far(c, way):
        half, land, r = ((first, half_up, above), (second, half_down, below))[way]
        return remote(
            far_part.at[half, bcols(c)],
            land.at[:, bcols(c)],
            h_send.at[c, way],
            h_recv.at[c, way],
            at(line, r),
        )

    def near(c, i):
        r, half, source, land = (
            (above, second, up_part, full_up),
            (below, first, down_part, full_down),
            (above, first, up_part, full_up),
            (below, second, down_part, full_down),
        )[i]
        return remote(
            source.at[half, bcols(c)],
            land.at[half, bcols(c)],
            f_send.at[c, i],
            f_recv.at[c, i],
            at(line, r),
        )

    def from_line(c, d, slot):
        g = turn(line, d)
        return remote(
            brows.at[rows_at(g, srows), bcols(c)],
            gback.at[rows_at(slot, srows), bcols(c)],
            gb_send.at[c, d],
            gb_recv.at[c, d],
            at(g, rank),
        )

    def b_out(c):
        return Exchange(
            "exp",
            lambda t: zback.at[rows_at(t, zrows), bcols(c)],
            lambda s: bland.at[rows_at(s, zrows), bcols(c)],
            b_send.at[c],
            b_recv.at[c],
        )

    def second_layer(c):
        def one(r):
            return jnp.dot(hidden[r], wout_land[:, bcols(c)], preferred_element_type=F32)

        far_part[:, bcols(c)] = one(across).astype(BF16)
        go(far(c, 0))
        go(far(c, 1))
        product = one(above)
        up_part[second, bcols(c)] = product[mid:].astype(BF16)
        go(near(c, 0))
        up_wait[:, bcols(c)] = product[:mid]
        product = one(below)
        down_part[first, bcols(c)] = product[:mid].astype(BF16)
        go(near(c, 1))
        down_wait[:, bcols(c)] = product[mid:]
        own_part[:, bcols(c)] = one(rank)

    def add_far(c):
        far(c, 0).wait_recv()
        up_part[first, bcols(c)] = (
            up_wait[:, bcols(c)] + half_up[:, bcols(c)].astype(F32)
        ).astype(BF16)
        go(near(c, 2))
        far(c, 1).wait_recv()
        down_part[second, bcols(c)] = (
            down_wait[:, bcols(c)] + half_down[:, bcols(c)].astype(F32)
        ).astype(BF16)
        go(near(c, 3))

    def finish(c):
        for i in (0, 1, 2, 3):
            near(c, i).wait_recv()
        brows[:, bcols(c)] = (
            own_part[:, bcols(c)]
            + full_up[:, bcols(c)].astype(F32)
            + full_down[:, bcols(c)].astype(F32)
        ).astype(BF16)
        for d in range(1, experts):
            go(from_line(c, d, line))
        gback[rows_at(line, srows), bcols(c)] = brows[rows_at(line, srows), bcols(c)]

    def give_back(c):
        for d in range(1, experts):
            from_line(c, d, turn(line, -d)).wait_recv()
        zback[:, bcols(c)] = jnp.dot(
            inverse, gback[:, bcols(c)], preferred_element_type=F32
        ).astype(BF16)
        go(b_out(c))
        bland[rows_at(exp, zrows), bcols(c)] = zback[rows_at(exp, zrows), bcols(c)]

    second_layer(0)
    add_far(0)
    for c in range(1, back_chunks):
        second_layer(c)
        finish(c - 1)
        add_far(c)
        give_back(c - 1)
    finish(back_chunks - 1)
    give_back(back_chunks - 1)

    q_own.wait()
    q_out.arrived()
    for c in range(back_chunks):
        b_out(c).arrived()
    back_ref[...] = bland[...]
    for transfer in started:
        transfer.wait_send()


def attend_kernel(
    rows_ref,
    wk_ref,
    wv_ref,
    q_ref,
    out_ref,
    kvsend,
    kvland,
    vland,
    qrows,
    csend,
    cland,
    k_send,
    k_recv,
    c_send,
    c_recv,
):
    seq = lax.axis_index("seq")
    n_seq = lax.axis_size("seq")
    count = rows_ref.shape[0]
    barrier, greeted = signal_all(("seq",))
    pl.semaphore_wait(barrier, greeted)
    lane = lax.broadcasted_iota(jnp.int32, (count, 128), 1)
    low = lane < 64
    block = rows_ref[...]
    for g in range(HEADS // 4):
        cols = slice(g * 256, (g + 1) * 256)
        keys = jnp.dot(block, wk_ref[:, cols], preferred_element_type=F32)
        values = jnp.dot(block, wv_ref[:, cols], preferred_element_type=F32)
        for i in range(2):
            k_pair = pltpu.roll(keys[:, i * 128 : (i + 1) * 128], 64, 1)
            v_pair = values[:, i * 128 : (i + 1) * 128]
            head = g * 4 + i * 2
            kvsend[head] = jnp.where(low, v_pair, k_pair).astype(BF16)
            kvsend[head + 1] = jnp.where(low, k_pair, v_pair).astype(BF16)
    kv_out = Exchange(
        "seq",
        lambda t: kvsend.at[t],
        lambda s: kvland.at[rows_at(s, count)],
        k_send,
        k_recv,
    )
    kv_out.start()
    kvland[rows_at(seq, count), :] = kvsend[seq]

    even = lax.rem(seq, 2) == 0
    q_half = q_ref.shape[1]
    q_count = 2 * q_half
    packed = q_ref[...].reshape(n_seq * q_half, 128).astype(F32)
    turned = pltpu.roll(packed, 64, 1)
    side = lax.broadcasted_iota(jnp.int32, packed.shape, 1)
    at_keys = jnp.where(even, side, side + 64) % 128 >= 64
    top = jnp.where(at_keys, jnp.where(even, turned, packed), 0.0).astype(BF16)
    bottom = jnp.where(at_keys, jnp.where(even, packed, turned), 0.0).astype(BF16)
    for t in range(n_seq):
        qrows[t * q_count : t * q_count + q_half, :] = top[t * q_half : (t + 1) * q_half]
        qrows[t * q_count + q_half : (t + 1) * q_count, :] = bottom[t * q_half : (t + 1) * q_half]
    kv_out.arrived()

    c_out = Exchange("seq", lambda t: csend.at[t], lambda s: cland.at[s], c_send, c_recv)

    wide_lane = lax.broadcasted_iota(jnp.int32, kvland.shape, 1)
    key_side = 64 * (1 - lax.rem(seq, 2))
    is_key = (wide_lane >= key_side) & (wide_lane < key_side + 64)
    vland[...] = jnp.where(is_key, jnp.ones((), BF16), kvland[...])
    pair_rows = 2 * q_count
    lane = lax.broadcasted_iota(jnp.int32, (q_half, 128), 1)
    at_values = jnp.where(even, lane, lane + 64) % 128 < 64

    def scores_of(i):
        return lax.dot_general(
            qrows[rows_at(i, pair_rows), :],
            kvland[...],
            (((1,), (1,)), ((), ())),
            preferred_element_type=F32,
        )

    def context_of(scores):
        expo = jnp.exp(scores - jnp.max(scores, axis=-1, keepdims=True))
        mixed = jnp.dot(expo.astype(BF16), vland[...], preferred_element_type=F32)
        context = mixed / pltpu.roll(mixed, 64, 1)
        turned = pltpu.roll(context, 64, 1)
        return [
            jnp.where(
                at_values, context[i : i + q_half], turned[i + q_half : i + q_count]
            ).astype(BF16)
            for i in range(0, pair_rows, q_count)
        ]

    group = 4

    def step(d, carry):
        g = lax.rem(seq // group + d, n_seq // group)
        both = [scores_of(2 * g + i) for i in range(2)]
        for i in range(2):
            for j, context in enumerate(context_of(both[i])):
                csend[g * group + 2 * i + j] = context
        for i in range(group):
            t = g * group + i

            @pl.when(t != seq)
            def _():
                c_out.start_one(lax.rem(t - seq + n_seq, n_seq))

        return carry

    lax.fori_loop(0, n_seq // group, step, 0)
    cland[seq] = csend[seq]
    c_out.arrived()
    for p in range(HEADS // 2):
        one, two = cland[2 * p].astype(F32), cland[2 * p + 1].astype(F32)
        out_ref[:q_half, p * 128 : (p + 1) * 128] = jnp.where(lane < 64, one, two).astype(BF16)
        out_ref[q_half:, p * 128 : (p + 1) * 128] = pltpu.roll(
            jnp.where(lane < 64, two, one), 64, 1
        ).astype(BF16)
    kv_out.wait_send()
    c_out.wait_send()


def per_device(
    enc_in,
    expert_ids,
    slots,
    expert_gate,
    moe_gain,
    w_in,
    w_out,
    final_gain,
    w_key,
    w_value,
    dec_query,
):
    n_exp, n_seq = lax.axis_size("exp"), lax.axis_size("seq")
    tok_rows, width = enc_in.shape[1:]
    experts, _, part_ff = w_in.shape
    capacity = tok_rows // (experts * n_exp)
    q_rows = dec_query.shape[1]

    vmem = pl.BlockSpec(memory_space=pltpu.VMEM)
    hbm = pl.BlockSpec(memory_space=pl.ANY)
    dma = pltpu.SemaphoreType.DMA
    whole = pltpu.VMEM((tok_rows, width), BF16)
    half = pltpu.VMEM((tok_rows // 2, width), BF16)
    weight = pltpu.VMEM((experts * part_ff, width), BF16)
    back, queries = pl.pallas_call(
        moe_kernel,
        out_shape=(
            jax.ShapeDtypeStruct((tok_rows, width), BF16),
            jax.ShapeDtypeStruct((n_seq, q_rows // 2, 128), BF16),
        ),
        in_specs=[hbm, vmem, vmem, vmem, hbm, hbm, hbm],
        out_specs=(vmem, hbm),
        scratch_shapes=[
            whole,
            pltpu.VMEM((q_rows, width), BF16),
            whole,
            whole,
            whole,
            pltpu.VMEM((experts, tok_rows, width), BF16),
            weight,
            weight,
            pltpu.VMEM((part_ff, width), BF16),
            pltpu.VMEM((experts, tok_rows, experts * part_ff), BF16),
            whole,
            whole,
            whole,
            pltpu.VMEM((tok_rows // 2, width), F32),
            pltpu.VMEM((tok_rows // 2, width), F32),
            pltpu.VMEM((tok_rows, width), F32),
            half,
            half,
            whole,
            whole,
            whole,
            whole,
            whole,
            whole,
            pltpu.VMEM((n_seq, q_rows // 2, 128), BF16),
            dma((4,)),
        ]
        + [dma((OUT_CHUNKS, n_exp))] * 2
        + [dma((BACK_CHUNKS, n_exp))] * 2
        + [dma((n_seq,))] * 2
        + [dma((experts,))] * 4
        + [dma((2,))] * 2
        + [dma((OUT_CHUNKS, experts))] * 8
        + [dma((BACK_CHUNKS, 2))] * 2
        + [dma((BACK_CHUNKS, 4))] * 2
        + [dma((BACK_CHUNKS, experts))] * 2,
        compiler_params=pltpu.CompilerParams(
            collective_id=0, has_side_effects=True, vmem_limit_bytes=56 << 20
        ),
        name="experts",
    )(
        enc_in[0],
        expert_ids,
        slots,
        moe_gain[None],
        jnp.swapaxes(w_in, 1, 2),
        w_out,
        dec_query[0],
    )

    inputs = enc_in[0].astype(F32)
    places = jnp.arange(tok_rows, dtype=jnp.int32)
    target = jnp.where(slots[0] < capacity, expert_ids[0] * capacity + slots[0], -1)
    combine = (target[:, None] == places[None, :]).astype(BF16)
    combined = jnp.dot(combine, back, preferred_element_type=F32)
    enc_rows = inputs + expert_gate[0][:, None] * combined
    enc_out = enc_rows.astype(BF16)
    kv_rows = rms_scale(enc_out.astype(F32), final_gain).astype(BF16)
    context = pl.pallas_call(
        attend_kernel,
        out_shape=jax.ShapeDtypeStruct((q_rows, width), BF16),
        in_specs=[vmem] * 4,
        out_specs=vmem,
        scratch_shapes=[
            pltpu.VMEM((n_seq, tok_rows, 128), BF16),
            pltpu.VMEM((n_seq * tok_rows, 128), BF16),
            pltpu.VMEM((n_seq * tok_rows, 128), BF16),
            pltpu.VMEM((n_seq * q_rows, 128), BF16),
            pltpu.VMEM((n_seq, q_rows // 2, 128), BF16),
            pltpu.VMEM((n_seq, q_rows // 2, 128), BF16),
        ]
        + [dma((n_seq,))] * 4,
        compiler_params=pltpu.CompilerParams(
            collective_id=1, has_side_effects=True, vmem_limit_bytes=40 << 20
        ),
        name="attend",
    )(kv_rows, w_key, w_value, queries)
    return (enc_out[None], context[None])


def solution(mesh):
    placed = (
        P("exp", "seq", None),
        P("exp", "seq"),
        P("exp", "seq"),
        P("exp", "seq"),
        P(),
        P("exp", None, "seq"),
        P("exp", "seq", None),
        P(),
        P(),
        P(),
        P("exp", "seq", None),
    )
    return jax.shard_map(
        per_device,
        mesh=mesh,
        in_specs=placed,
        out_specs=(P("exp", "seq", None), P("exp", "seq", None)),
        check_vma=False,
    )
```

```python
import functools

import jax
import jax.numpy as jnp
from jax import lax
from jax.experimental import pallas as pl
from jax.experimental.pallas import tpu as pltpu
from jax.sharding import PartitionSpec as P

HEADS = 16
OUT_CHUNKS = 1
BACK_CHUNKS = 2
KEY_GROUPS = 2
MESH = pl.DeviceIdType.MESH
F32 = jnp.float32
BF16 = jnp.bfloat16


def rms_scale(values, gain):
    mean_square = jnp.mean(values * values, axis=-1, keepdims=True)
    return values * lax.rsqrt(mean_square + 1e-06) * gain


def rows_at(index, count):
    return pl.ds(pl.multiple_of(index * count, count), count)


def signal_all(axes):
    barrier = pltpu.get_barrier_semaphore()
    total = 0
    for axis in axes:
        n = lax.axis_size(axis)
        me = lax.axis_index(axis)
        total += n - 1

        def signal(d, carry, axis=axis, n=n, me=me):
            pl.semaphore_signal(
                barrier, inc=1, device_id={axis: lax.rem(me + d, n)}, device_id_type=MESH
            )
            return carry

        lax.fori_loop(1, n, signal, 0)
    return barrier, total


class Exchange:
    def __init__(self, axis, source, landing, send, recv, by_step=False):
        self.by_step = by_step
        self.axis, self.source, self.landing = axis, source, landing
        self.send, self.recv = send, recv
        self.n, self.me = lax.axis_size(axis), lax.axis_index(axis)

    def copy(self, d, slot):
        t = lax.rem(self.me + d, self.n)
        return pltpu.make_async_remote_copy(
            src_ref=self.source(t),
            dst_ref=self.landing(slot),
            send_sem=self.send.at[d],
            recv_sem=self.recv.at[d],
            device_id={self.axis: t},
            device_id_type=MESH,
        )

    def start_one(self, d):
        self.copy(d, d if self.by_step else self.me).start()

    def wait_one(self, d):
        slot = d if self.by_step else lax.rem(self.me + self.n - d, self.n)
        self.copy(d, slot).wait_recv()

    def loop(self, act, first=1, last=None):
        def body(d, carry):
            act(d)
            return carry

        lax.fori_loop(first, self.n if last is None else last, body, 0)

    def start(self):
        self.loop(self.start_one)

    def arrived(self, first=1, last=None):
        self.loop(self.wait_one, first, last)

    def wait_send(self):
        self.loop(lambda d: self.copy(d, self.me).wait_send())


def remote(src, dst, send, recv, seq):
    return pltpu.make_async_remote_copy(
        src_ref=src,
        dst_ref=dst,
        send_sem=send,
        recv_sem=recv,
        device_id={"seq": seq},
        device_id_type=MESH,
    )


def layer_kernel(
    enc_ref,
    ids_ref,
    slots_ref,
    gate_ref,
    gain_ref,
    win_ref,
    wout_ref,
    final_gain_ref,
    wk_ref,
    wv_ref,
    q_ref,
    enc_out_ref,
    out_ref,
    enc,
    query,
    place,
    w_key,
    w_value,
    packed,
    zland,
    rows,
    rland,
    win_land,
    wout_land,
    hidden,
    far_part,
    up_part,
    down_part,
    up_wait,
    down_wait,
    own_part,
    half_up,
    half_down,
    full_up,
    full_down,
    brows,
    gback,
    zback,
    bland,
    qsend,
    qland,
    qrows,
    kvsend,
    kvland,
    vland,
    sums,
    peaks,
    csend,
    cland,
    local_sem,
    z_send,
    z_recv,
    b_send,
    b_recv,
    q_send,
    q_recv,
    wi_send,
    wi_recv,
    wo_send,
    wo_recv,
    g_send,
    g_recv,
    up_send,
    up_recv,
    down_send,
    down_recv,
    fwd_send,
    fwd_recv,
    h_send,
    h_recv,
    f_send,
    f_recv,
    gb_send,
    gb_recv,
    k_send,
    k_recv,
    c_send,
    c_recv,
):
    seq, exp = lax.axis_index("seq"), lax.axis_index("exp")
    n_seq, n_exp = lax.axis_size("seq"), lax.axis_size("exp")
    experts = win_ref.shape[0]
    hidden_part = win_ref.shape[1]
    tok = enc_ref.shape[0]
    zrows, srows = tok // n_exp, tok // experts
    capacity = zrows // experts
    core = lax.rem(exp, 2)
    y, x = seq // experts, lax.rem(seq, experts)
    line, rank = y + core * (x - y), x + core * (y - x)

    def at(g, r):
        return g * (experts - core * (experts - 1)) + r * (1 + core * (experts - 1))

    def turn(value, d):
        return lax.rem(value + experts + d, experts)

    enc_in = pltpu.make_async_copy(enc_ref, enc, local_sem.at[0])
    q_in = pltpu.make_async_copy(q_ref, query, local_sem.at[1])
    enc_in.start()
    q_in.start()
    barrier, greeted = signal_all(("seq", "exp"))
    projections = [
        pltpu.make_async_copy(ref, land, local_sem.at[4 + i])
        for i, (ref, land) in enumerate(((wk_ref, w_key), (wv_ref, w_value)))
    ]
    own_weights = [
        pltpu.make_async_copy(
            ref.at[line], land.at[rows_at(line, hidden_part)], local_sem.at[2 + i]
        )
        for i, (ref, land) in enumerate(((win_ref, win_land), (wout_ref, wout_land)))
    ]
    for copy in own_weights:
        copy.start()
    enc_in.wait()
    normed = rms_scale(enc[...].astype(F32), gain_ref[...]).astype(BF16)
    target = jnp.where(slots_ref[...] < capacity, ids_ref[...] * capacity + slots_ref[...], -1)
    out_row = lax.broadcasted_iota(jnp.int32, (tok, tok), 0)
    in_row = lax.broadcasted_iota(jnp.int32, (tok, tok), 1)
    place[...] = (out_row == target).astype(BF16)
    packed[...] = jnp.dot(place[...], normed, preferred_element_type=F32).astype(BF16)
    q_in.wait()
    q_half = q_ref.shape[0] // 2
    lane = lax.broadcasted_iota(jnp.int32, (q_half, 128), 1)
    for p in range(HEADS // 2):
        pair = query[:, p * 128 : (p + 1) * 128].astype(F32) * 0.125
        turned = pltpu.roll(pair, 64, 1)
        qsend[2 * p] = jnp.where(lane < 64, pair[:q_half], turned[q_half:]).astype(BF16)
        qsend[2 * p + 1] = jnp.where(lane < 64, turned[:q_half], pair[q_half:]).astype(BF16)
    pl.semaphore_wait(barrier, greeted)

    started = []

    def go(transfer):
        transfer.start()
        started.append(transfer)

    chunks, back_chunks = z_send.shape[0], b_send.shape[0]
    wide = enc_ref.shape[1] // chunks
    back_wide = enc_ref.shape[1] // back_chunks

    def cols(c):
        return pl.ds(c * wide, wide)

    def bcols(c):
        return pl.ds(c * back_wide, back_wide)

    def z_out(c):
        return Exchange(
            "exp",
            lambda t: packed.at[rows_at(t, zrows), cols(c)],
            lambda s: zland.at[rows_at(s, zrows), cols(c)],
            z_send.at[c],
            z_recv.at[c],
        )

    def weight_copy(d, slot, ref, land, send, recv):
        k = turn(line, d)
        return remote(
            ref.at[k], land.at[rows_at(slot, hidden_part)], send.at[d], recv.at[d], at(k, rank)
        )

    w_first = (win_ref, win_land, wi_send, wi_recv)
    w_second = (wout_ref, wout_land, wo_send, wo_recv)
    direct = [(d, w_first) for d in range(1, experts)] + [(d, w_second) for d in range(1, experts)]
    go(z_out(0))
    for d, each in direct:
        go(weight_copy(d, line, *each))
    for c in range(1, chunks):
        go(z_out(c))
    for copy in projections:
        copy.start()
    zland[rows_at(exp, zrows), :] = packed[rows_at(exp, zrows), :]

    def by_expert(r):
        j, k, c = r // zrows, lax.rem(r // capacity, experts), lax.rem(r, capacity)
        return k * srows + j * capacity + c

    forward = (by_expert(in_row) == out_row).astype(BF16)
    inverse = (by_expert(out_row) == in_row).astype(BF16)

    above, below, across = turn(rank, 1), turn(rank, -1), turn(rank, 2)

    def piece(r, g, c):
        return rland.at[r, rows_at(g, srows), cols(c)]

    def to_line(c, d, slot):
        k = turn(line, d)
        return remote(
            rows.at[rows_at(k, srows), cols(c)],
            piece(rank, slot, c),
            g_send.at[c, d],
            g_recv.at[c, d],
            at(k, rank),
        )

    def up(c, d, r):
        g = turn(line, -d)
        return remote(
            piece(rank, g, c), piece(r, g, c), up_send.at[c, d], up_recv.at[c, d], at(line, above)
        )

    def down(c, d, r):
        g = turn(line, -d)
        return remote(
            piece(rank, g, c),
            piece(r, g, c),
            down_send.at[c, d],
            down_recv.at[c, d],
            at(line, below),
        )

    def forwarded(c, d, r):
        g = turn(line, -d)
        way = 1 if d < 2 else -1
        return remote(
            piece(turn(rank, -way), g, c),
            piece(r, g, c),
            fwd_send.at[c, d],
            fwd_recv.at[c, d],
            at(line, turn(rank, way)),
        )

    for c in range(chunks):
        z_out(c).arrived()
        rows[:, cols(c)] = jnp.dot(
            forward, zland[:, cols(c)], preferred_element_type=F32
        ).astype(BF16)
        for d in range(1, experts):
            go(to_line(c, d, line))
        rland[rank, rows_at(line, srows), cols(c)] = rows[rows_at(line, srows), cols(c)]
        for d in range(experts):
            if d:
                to_line(c, d, turn(line, -d)).wait_recv()
            go(up(c, d, rank))
            go(down(c, d, rank))
        for d in (0, 1):
            up(c, d, below).wait_recv()
            go(forwarded(c, d, below))
        for d in (2, 3):
            down(c, d, above).wait_recv()
            go(forwarded(c, d, above))

    def first_layer(r):
        product = lax.dot_general(
            rland[r], win_land[...], (((1,), (1,)), ((), ())), preferred_element_type=F32
        )
        hidden[r] = jnp.maximum(product, 0.0).astype(BF16)

    for copy in own_weights:
        copy.wait()
    for d, each in direct:
        if each is w_first:
            weight_copy(d, turn(line, -d), *each).wait_recv()
    first_layer(rank)
    for c in range(chunks):
        for d in (2, 3):
            up(c, d, below).wait_recv()
    first_layer(below)
    for c in range(chunks):
        for d in (0, 1):
            down(c, d, above).wait_recv()
    first_layer(above)
    for c in range(chunks):
        for d in range(experts):
            forwarded(c, d, across).wait_recv()
    first_layer(across)
    for d, each in direct:
        if each is w_second:
            weight_copy(d, turn(line, -d), *each).wait_recv()

    mid = tok // 2
    first, second = pl.ds(0, mid), pl.ds(mid, mid)

    def far(c, way):
        half, land, r = ((first, half_up, above), (second, half_down, below))[way]
        return remote(
            far_part.at[half, bcols(c)],
            land.at[:, bcols(c)],
            h_send.at[c, way],
            h_recv.at[c, way],
            at(line, r),
        )

    def near(c, i):
        r, half, source, land = (
            (above, second, up_part, full_up),
            (below, first, down_part, full_down),
            (above, first, up_part, full_up),
            (below, second, down_part, full_down),
        )[i]
        return remote(
            source.at[half, bcols(c)],
            land.at[half, bcols(c)],
            f_send.at[c, i],
            f_recv.at[c, i],
            at(line, r),
        )

    def from_line(c, d, slot):
        g = turn(line, d)
        return remote(
            brows.at[rows_at(g, srows), bcols(c)],
            gback.at[rows_at(slot, srows), bcols(c)],
            gb_send.at[c, d],
            gb_recv.at[c, d],
            at(g, rank),
        )

    def b_out(c):
        return Exchange(
            "exp",
            lambda t: zback.at[rows_at(t, zrows), bcols(c)],
            lambda s: bland.at[rows_at(s, zrows), bcols(c)],
            b_send.at[c],
            b_recv.at[c],
        )

    def second_layer(c):
        def one(r):
            return jnp.dot(hidden[r], wout_land[:, bcols(c)], preferred_element_type=F32)

        far_part[:, bcols(c)] = one(across).astype(BF16)
        go(far(c, 0))
        go(far(c, 1))
        product = one(above)
        up_part[second, bcols(c)] = product[mid:].astype(BF16)
        go(near(c, 0))
        up_wait[:, bcols(c)] = product[:mid]
        product = one(below)
        down_part[first, bcols(c)] = product[:mid].astype(BF16)
        go(near(c, 1))
        down_wait[:, bcols(c)] = product[mid:]
        own_part[:, bcols(c)] = one(rank)

    def add_far(c):
        far(c, 0).wait_recv()
        up_part[first, bcols(c)] = (
            up_wait[:, bcols(c)] + half_up[:, bcols(c)].astype(F32)
        ).astype(BF16)
        go(near(c, 2))
        far(c, 1).wait_recv()
        down_part[second, bcols(c)] = (
            down_wait[:, bcols(c)] + half_down[:, bcols(c)].astype(F32)
        ).astype(BF16)
        go(near(c, 3))

    def finish(c):
        for i in (0, 1, 2, 3):
            near(c, i).wait_recv()
        brows[:, bcols(c)] = (
            own_part[:, bcols(c)]
            + full_up[:, bcols(c)].astype(F32)
            + full_down[:, bcols(c)].astype(F32)
        ).astype(BF16)
        for d in range(1, experts):
            go(from_line(c, d, line))
        gback[rows_at(line, srows), bcols(c)] = brows[rows_at(line, srows), bcols(c)]

    def give_back(c):
        for d in range(1, experts):
            from_line(c, d, turn(line, -d)).wait_recv()
        zback[:, bcols(c)] = jnp.dot(
            inverse, gback[:, bcols(c)], preferred_element_type=F32
        ).astype(BF16)
        go(b_out(c))
        bland[rows_at(exp, zrows), bcols(c)] = zback[rows_at(exp, zrows), bcols(c)]

    second_layer(0)
    add_far(0)
    for c in range(1, back_chunks):
        second_layer(c)
        finish(c - 1)
        add_far(c)
        give_back(c - 1)
    finish(back_chunks - 1)
    give_back(back_chunks - 1)

    q_out = Exchange(
        "seq", lambda t: qsend.at[t], lambda s: qland.at[s], q_send, q_recv
    )
    go(q_out)
    qland[seq] = qsend[seq]

    diagonal = out_row == in_row
    gate = jnp.sum(jnp.where(diagonal, gate_ref[...], 0.0), axis=1, keepdims=True)
    for c in range(back_chunks):
        b_out(c).arrived()
        combined = lax.dot_general(
            place[...], bland[:, bcols(c)], (((0,), (0,)), ((), ())), preferred_element_type=F32
        )
        enc_out_ref[:, bcols(c)] = (enc[:, bcols(c)].astype(F32) + gate * combined).astype(BF16)
    block = rms_scale(enc_out_ref[...].astype(F32), final_gain_ref[...]).astype(BF16)
    for copy in projections:
        copy.wait()
    lane = lax.broadcasted_iota(jnp.int32, (tok, 128), 1)
    low = lane < 64
    for g in range(HEADS // 4):
        span = slice(g * 256, (g + 1) * 256)
        keys = jnp.dot(block, w_key[:, span], preferred_element_type=F32)
        values = jnp.dot(block, w_value[:, span], preferred_element_type=F32)
        for i in range(2):
            k_pair = pltpu.roll(keys[:, i * 128 : (i + 1) * 128], 64, 1)
            v_pair = values[:, i * 128 : (i + 1) * 128]
            head = g * 4 + i * 2
            kvsend[head] = jnp.where(low, v_pair, k_pair).astype(BF16)
            kvsend[head + 1] = jnp.where(low, k_pair, v_pair).astype(BF16)
    kv_out = Exchange(
        "seq",
        lambda t: kvsend.at[t],
        lambda s: kvland.at[rows_at(s, tok)],
        k_send,
        k_recv,
        by_step=True,
    )
    go(kv_out)
    kvland[0:tok, :] = kvsend[seq]

    q_out.arrived()
    even = lax.rem(seq, 2) == 0
    q_count = 2 * q_half
    folded = qland[...].reshape(n_seq * q_half, 128).astype(F32)
    turned = pltpu.roll(folded, 64, 1)
    side = lax.broadcasted_iota(jnp.int32, folded.shape, 1)
    at_keys = jnp.where(even, side, side + 64) % 128 >= 64
    top = jnp.where(at_keys, jnp.where(even, turned, folded), 0.0).astype(BF16)
    bottom = jnp.where(at_keys, jnp.where(even, folded, turned), 0.0).astype(BF16)
    for t in range(n_seq):
        qrows[t * q_count : t * q_count + q_half, :] = top[t * q_half : (t + 1) * q_half]
        qrows[t * q_count + q_half : (t + 1) * q_count, :] = bottom[t * q_half : (t + 1) * q_half]

    c_out = Exchange("seq", lambda t: csend.at[t], lambda s: cland.at[s], c_send, c_recv)
    span_rows = kvland.shape[0] // KEY_GROUPS
    wide_lane = lax.broadcasted_iota(jnp.int32, (span_rows, 128), 1)
    is_key = jnp.where(even, wide_lane, wide_lane + 64) % 128 >= 64
    pair_rows = 2 * q_count
    lane = lax.broadcasted_iota(jnp.int32, (q_half, 128), 1)
    at_values = jnp.where(even, lane, lane + 64) % 128 < 64
    group = 4

    def attend(part, last):
        span = slice(part * span_rows, (part + 1) * span_rows)
        per = span_rows // tok
        kv_out.arrived(max(1, part * per), (part + 1) * per)
        vland[span, :] = jnp.where(is_key, jnp.ones((), BF16), kvland[span, :])

        def step(d, carry):
            g = lax.rem(seq // group + d, n_seq // group)
            tiles = [rows_at(2 * g + i, pair_rows) for i in range(2)]
            both = [
                lax.dot_general(
                    qrows[tile, :],
                    kvland[span, :],
                    (((1,), (1,)), ((), ())),
                    preferred_element_type=F32,
                )
                for tile in tiles
            ]
            for i, tile in enumerate(tiles):
                peak = jnp.max(both[i], axis=-1, keepdims=True)
                if part:
                    old = peaks[tile, 0:1]
                    peak = jnp.maximum(peak, old)
                expo = jnp.exp(both[i] - peak).astype(BF16)
                mixed = jnp.dot(expo, vland[span, :], preferred_element_type=F32)
                if part:
                    mixed = mixed + jnp.exp(old - peak) * sums[tile, :]
                if not last:
                    sums[tile, :] = mixed
                    peaks[tile, :] = jnp.broadcast_to(peak, mixed.shape)
                    continue
                context = mixed / pltpu.roll(mixed, 64, 1)
                turned = pltpu.roll(context, 64, 1)
                for j in range(2):
                    k = j * q_count
                    csend[g * group + 2 * i + j] = jnp.where(
                        at_values, context[k : k + q_half], turned[k + q_half : k + q_count]
                    ).astype(BF16)
            if last:
                for i in range(group):
                    t = g * group + i

                    @pl.when(t != seq)
                    def _():
                        c_out.start_one(lax.rem(t - seq + n_seq, n_seq))

            return carry

        lax.fori_loop(0, n_seq // group, step, 0)

    for part in range(KEY_GROUPS):
        attend(part, part == KEY_GROUPS - 1)
    started.append(c_out)
    cland[seq] = csend[seq]
    c_out.arrived()
    for p in range(HEADS // 2):
        one, two = cland[2 * p].astype(F32), cland[2 * p + 1].astype(F32)
        out_ref[:q_half, p * 128 : (p + 1) * 128] = jnp.where(lane < 64, one, two).astype(BF16)
        out_ref[q_half:, p * 128 : (p + 1) * 128] = pltpu.roll(
            jnp.where(lane < 64, two, one), 64, 1
        ).astype(BF16)
    for transfer in started:
        transfer.wait_send()


def per_device(
    enc_in,
    expert_ids,
    slots,
    expert_gate,
    moe_gain,
    w_in,
    w_out,
    final_gain,
    w_key,
    w_value,
    dec_query,
):
    n_exp, n_seq = lax.axis_size("exp"), lax.axis_size("seq")
    tok_rows, width = enc_in.shape[1:]
    experts, _, part_ff = w_in.shape
    q_rows = dec_query.shape[1]

    vmem = pl.BlockSpec(memory_space=pltpu.VMEM)
    hbm = pl.BlockSpec(memory_space=pl.ANY)
    dma = pltpu.SemaphoreType.DMA
    whole = pltpu.VMEM((tok_rows, width), BF16)
    half = pltpu.VMEM((tok_rows // 2, width), BF16)
    weight = pltpu.VMEM((experts * part_ff, width), BF16)
    square = pltpu.VMEM((width, width), BF16)
    folded = pltpu.VMEM((n_seq, q_rows // 2, 128), BF16)
    enc_out, context = pl.pallas_call(
        layer_kernel,
        out_shape=(
            jax.ShapeDtypeStruct((tok_rows, width), BF16),
            jax.ShapeDtypeStruct((q_rows, width), BF16),
        ),
        in_specs=[hbm, vmem, vmem, vmem, vmem, hbm, hbm, vmem, hbm, hbm, hbm],
        out_specs=(vmem, vmem),
        scratch_shapes=[
            whole,
            pltpu.VMEM((q_rows, width), BF16),
            pltpu.VMEM((tok_rows, tok_rows), BF16),
            square,
            square,
            whole,
            whole,
            whole,
            pltpu.VMEM((experts, tok_rows, width), BF16),
            weight,
            weight,
            pltpu.VMEM((experts, tok_rows, experts * part_ff), BF16),
            whole,
            whole,
            whole,
            pltpu.VMEM((tok_rows // 2, width), F32),
            pltpu.VMEM((tok_rows // 2, width), F32),
            pltpu.VMEM((tok_rows, width), F32),
            half,
            half,
            whole,
            whole,
            whole,
            whole,
            whole,
            whole,
            folded,
            folded,
            pltpu.VMEM((n_seq * q_rows, 128), BF16),
            pltpu.VMEM((n_seq, tok_rows, 128), BF16),
            pltpu.VMEM((n_seq * tok_rows, 128), BF16),
            pltpu.VMEM((n_seq * tok_rows, 128), BF16),
            pltpu.VMEM((n_seq * q_rows, 128), F32),
            pltpu.VMEM((n_seq * q_rows, 128), F32),
            folded,
            folded,
            dma((6,)),
        ]
        + [dma((OUT_CHUNKS, n_exp))] * 2
        + [dma((BACK_CHUNKS, n_exp))] * 2
        + [dma((n_seq,))] * 2
        + [dma((experts,))] * 4
        + [dma((OUT_CHUNKS, experts))] * 8
        + [dma((BACK_CHUNKS, 2))] * 2
        + [dma((BACK_CHUNKS, 4))] * 2
        + [dma((BACK_CHUNKS, experts))] * 2
        + [dma((n_seq,))] * 4,
        compiler_params=pltpu.CompilerParams(
            collective_id=0, has_side_effects=True, vmem_limit_bytes=56 << 20
        ),
        name="layer",
    )(
        enc_in[0],
        expert_ids,
        slots,
        expert_gate,
        moe_gain[None],
        jnp.swapaxes(w_in, 1, 2),
        w_out,
        final_gain[None],
        w_key,
        w_value,
        dec_query[0],
    )
    return (enc_out[None], context[None])


def solution(mesh):
    placed = (
        P("exp", "seq", None),
        P("exp", "seq"),
        P("exp", "seq"),
        P("exp", "seq"),
        P(),
        P("exp", None, "seq"),
        P("exp", "seq", None),
        P(),
        P(),
        P(),
        P("exp", "seq", None),
    )
    return jax.shard_map(
        per_device,
        mesh=mesh,
        in_specs=placed,
        out_specs=(P("exp", "seq", None), P("exp", "seq", None)),
        check_vma=False,
    )
```

```python
import functools

import jax
import jax.numpy as jnp
from jax import lax
from jax.experimental import pallas as pl
from jax.experimental.pallas import tpu as pltpu
from jax.sharding import PartitionSpec as P

HEADS = 16
OUT_CHUNKS = 1
BACK_CHUNKS = 2
KEY_GROUPS = 2
MESH = pl.DeviceIdType.MESH
F32 = jnp.float32
BF16 = jnp.bfloat16


def rms_scale(values, gain):
    mean_square = jnp.mean(values * values, axis=-1, keepdims=True)
    return values * lax.rsqrt(mean_square + 1e-06) * gain


def rows_at(index, count):
    return pl.ds(pl.multiple_of(index * count, count), count)


def signal_all(axes):
    barrier = pltpu.get_barrier_semaphore()
    total = 0
    for axis in axes:
        n = lax.axis_size(axis)
        me = lax.axis_index(axis)
        total += n - 1

        def signal(d, carry, axis=axis, n=n, me=me):
            pl.semaphore_signal(
                barrier, inc=1, device_id={axis: lax.rem(me + d, n)}, device_id_type=MESH
            )
            return carry

        lax.fori_loop(1, n, signal, 0)
    return barrier, total


class Exchange:
    def __init__(self, axis, source, landing, send, recv, route=None):
        self.route, self.by_step = route, route is not None
        self.axis, self.source, self.landing = axis, source, landing
        self.send, self.recv = send, recv
        self.n, self.me = lax.axis_size(axis), lax.axis_index(axis)

    def copy(self, d, slot):
        t = self.route(d) if self.route else lax.rem(self.me + d, self.n)
        return pltpu.make_async_remote_copy(
            src_ref=self.source(t),
            dst_ref=self.landing(slot),
            send_sem=self.send.at[d],
            recv_sem=self.recv.at[d],
            device_id={self.axis: t},
            device_id_type=MESH,
        )

    def start_one(self, d):
        self.copy(d, d if self.by_step else self.me).start()

    def wait_one(self, d):
        slot = d if self.by_step else lax.rem(self.me + self.n - d, self.n)
        self.copy(d, slot).wait_recv()

    def loop(self, act, first=1, last=None):
        def body(d, carry):
            act(d)
            return carry

        lax.fori_loop(first, self.n if last is None else last, body, 0)

    def start(self, first=1, last=None):
        self.loop(self.start_one, first, last)

    def arrived(self, first=1, last=None):
        self.loop(self.wait_one, first, last)

    def send_one(self, d):
        self.copy(d, self.me).wait_send()

    def wait_send(self):
        self.loop(lambda d: self.copy(d, self.me).wait_send())


def remote(src, dst, send, recv, seq):
    return pltpu.make_async_remote_copy(
        src_ref=src,
        dst_ref=dst,
        send_sem=send,
        recv_sem=recv,
        device_id={"seq": seq},
        device_id_type=MESH,
    )


def layer_kernel(
    enc_ref,
    ids_ref,
    slots_ref,
    gate_ref,
    gain_ref,
    win_ref,
    wout_ref,
    final_gain_ref,
    wk_ref,
    wv_ref,
    q_ref,
    enc_out_ref,
    out_ref,
    enc,
    query,
    place,
    w_key,
    w_value,
    packed,
    zland,
    rows,
    rland,
    win_land,
    wout_land,
    hidden,
    far_part,
    up_part,
    down_part,
    up_wait,
    down_wait,
    own_part,
    half_up,
    half_down,
    full_up,
    full_down,
    brows,
    gback,
    zback,
    bland,
    qsend,
    qland,
    qrows,
    kvsend,
    kvland,
    vland,
    sums,
    peaks,
    csend,
    cland,
    local_sem,
    z_send,
    z_recv,
    b_send,
    b_recv,
    q_send,
    q_recv,
    wi_send,
    wi_recv,
    wo_send,
    wo_recv,
    g_send,
    g_recv,
    up_send,
    up_recv,
    down_send,
    down_recv,
    fwd_send,
    fwd_recv,
    h_send,
    h_recv,
    f_send,
    f_recv,
    gb_send,
    gb_recv,
    k_send,
    k_recv,
    c_send,
    c_recv,
):
    seq, exp = lax.axis_index("seq"), lax.axis_index("exp")
    n_seq, n_exp = lax.axis_size("seq"), lax.axis_size("exp")
    experts = win_ref.shape[0]
    hidden_part = win_ref.shape[1]
    tok = enc_ref.shape[0]
    zrows, srows = tok // n_exp, tok // experts
    capacity = zrows // experts
    core = lax.rem(exp, 2)
    y, x = seq // experts, lax.rem(seq, experts)
    line, rank = y + core * (x - y), x + core * (y - x)

    def at(g, r):
        return g * (experts - core * (experts - 1)) + r * (1 + core * (experts - 1))

    def turn(value, d):
        return lax.rem(value + experts + d, experts)

    enc_in = pltpu.make_async_copy(enc_ref, enc, local_sem.at[0])
    q_in = pltpu.make_async_copy(q_ref, query, local_sem.at[1])
    enc_in.start()
    q_in.start()
    barrier, greeted = signal_all(("seq", "exp"))
    projections = [
        pltpu.make_async_copy(ref, land, local_sem.at[4 + i])
        for i, (ref, land) in enumerate(((wk_ref, w_key), (wv_ref, w_value)))
    ]
    own_weights = [
        pltpu.make_async_copy(
            ref.at[line], land.at[rows_at(line, hidden_part)], local_sem.at[2 + i]
        )
        for i, (ref, land) in enumerate(((win_ref, win_land), (wout_ref, wout_land)))
    ]
    for copy in own_weights:
        copy.start()
    enc_in.wait()
    normed = rms_scale(enc[...].astype(F32), gain_ref[...]).astype(BF16)
    target = jnp.where(slots_ref[...] < capacity, ids_ref[...] * capacity + slots_ref[...], -1)
    out_row = lax.broadcasted_iota(jnp.int32, (tok, tok), 0)
    in_row = lax.broadcasted_iota(jnp.int32, (tok, tok), 1)
    place[...] = (out_row == target).astype(BF16)
    packed[...] = jnp.dot(place[...], normed, preferred_element_type=F32).astype(BF16)
    q_in.wait()
    q_half = q_ref.shape[0] // 2
    lane = lax.broadcasted_iota(jnp.int32, (q_half, 128), 1)
    for p in range(HEADS // 2):
        pair = query[:, p * 128 : (p + 1) * 128].astype(F32) * 0.125
        turned = pltpu.roll(pair, 64, 1)
        qsend[2 * p] = jnp.where(lane < 64, pair[:q_half], turned[q_half:]).astype(BF16)
        qsend[2 * p + 1] = jnp.where(lane < 64, turned[:q_half], pair[q_half:]).astype(BF16)
    pl.semaphore_wait(barrier, greeted)

    started = []

    def go(transfer):
        transfer.start()
        started.append(transfer)

    chunks, back_chunks = z_send.shape[0], b_send.shape[0]
    wide = enc_ref.shape[1] // chunks
    back_wide = enc_ref.shape[1] // back_chunks

    def cols(c):
        return pl.ds(c * wide, wide)

    def bcols(c):
        return pl.ds(c * back_wide, back_wide)

    def z_out(c):
        return Exchange(
            "exp",
            lambda t: packed.at[rows_at(t, zrows), cols(c)],
            lambda s: zland.at[rows_at(s, zrows), cols(c)],
            z_send.at[c],
            z_recv.at[c],
        )

    def weight_copy(d, slot, ref, land, send, recv):
        k = turn(line, d)
        return remote(
            ref.at[k], land.at[rows_at(slot, hidden_part)], send.at[d], recv.at[d], at(k, rank)
        )

    w_first = (win_ref, win_land, wi_send, wi_recv)
    w_second = (wout_ref, wout_land, wo_send, wo_recv)
    direct = [(d, w_first) for d in range(1, experts)] + [(d, w_second) for d in range(1, experts)]
    go(z_out(0))
    for d, each in direct:
        go(weight_copy(d, line, *each))
    for c in range(1, chunks):
        go(z_out(c))
    for copy in projections:
        copy.start()
    zland[rows_at(exp, zrows), :] = packed[rows_at(exp, zrows), :]

    def by_expert(r):
        j, k, c = r // zrows, lax.rem(r // capacity, experts), lax.rem(r, capacity)
        return k * srows + j * capacity + c

    forward = (by_expert(in_row) == out_row).astype(BF16)
    inverse = (by_expert(out_row) == in_row).astype(BF16)

    above, below, across = turn(rank, 1), turn(rank, -1), turn(rank, 2)

    def piece(r, g, c):
        return rland.at[r, rows_at(g, srows), cols(c)]

    def to_line(c, d, slot):
        k = turn(line, d)
        return remote(
            rows.at[rows_at(k, srows), cols(c)],
            piece(rank, slot, c),
            g_send.at[c, d],
            g_recv.at[c, d],
            at(k, rank),
        )

    def up(c, d, r):
        g = turn(line, -d)
        return remote(
            piece(rank, g, c), piece(r, g, c), up_send.at[c, d], up_recv.at[c, d], at(line, above)
        )

    def down(c, d, r):
        g = turn(line, -d)
        return remote(
            piece(rank, g, c),
            piece(r, g, c),
            down_send.at[c, d],
            down_recv.at[c, d],
            at(line, below),
        )

    def forwarded(c, d, r):
        g = turn(line, -d)
        way = 1 if d < 2 else -1
        return remote(
            piece(turn(rank, -way), g, c),
            piece(r, g, c),
            fwd_send.at[c, d],
            fwd_recv.at[c, d],
            at(line, turn(rank, way)),
        )

    for c in range(chunks):
        z_out(c).arrived()
        rows[:, cols(c)] = jnp.dot(
            forward, zland[:, cols(c)], preferred_element_type=F32
        ).astype(BF16)
        for d in range(1, experts):
            go(to_line(c, d, line))
        rland[rank, rows_at(line, srows), cols(c)] = rows[rows_at(line, srows), cols(c)]
        for d in range(experts):
            if d:
                to_line(c, d, turn(line, -d)).wait_recv()
            go(up(c, d, rank))
            go(down(c, d, rank))
        for d in (0, 1):
            up(c, d, below).wait_recv()
            go(forwarded(c, d, below))
        for d in (2, 3):
            down(c, d, above).wait_recv()
            go(forwarded(c, d, above))

    def first_layer(r):
        product = lax.dot_general(
            rland[r], win_land[...], (((1,), (1,)), ((), ())), preferred_element_type=F32
        )
        hidden[r] = jnp.maximum(product, 0.0).astype(BF16)

    for copy in own_weights:
        copy.wait()
    for d, each in direct:
        if each is w_first:
            weight_copy(d, turn(line, -d), *each).wait_recv()
    first_layer(rank)
    for c in range(chunks):
        for d in (2, 3):
            up(c, d, below).wait_recv()
    first_layer(below)
    for c in range(chunks):
        for d in (0, 1):
            down(c, d, above).wait_recv()
    first_layer(above)
    for c in range(chunks):
        for d in range(experts):
            forwarded(c, d, across).wait_recv()
    first_layer(across)
    for d, each in direct:
        if each is w_second:
            weight_copy(d, turn(line, -d), *each).wait_recv()

    mid = tok // 2
    first, second = pl.ds(0, mid), pl.ds(mid, mid)

    def far(c, way):
        half, land, r = ((first, half_up, above), (second, half_down, below))[way]
        return remote(
            far_part.at[half, bcols(c)],
            land.at[:, bcols(c)],
            h_send.at[c, way],
            h_recv.at[c, way],
            at(line, r),
        )

    def near(c, i):
        r, half, source, land = (
            (above, second, up_part, full_up),
            (below, first, down_part, full_down),
            (above, first, up_part, full_up),
            (below, second, down_part, full_down),
        )[i]
        return remote(
            source.at[half, bcols(c)],
            land.at[half, bcols(c)],
            f_send.at[c, i],
            f_recv.at[c, i],
            at(line, r),
        )

    def from_line(c, d, slot):
        g = turn(line, d)
        return remote(
            brows.at[rows_at(g, srows), bcols(c)],
            gback.at[rows_at(slot, srows), bcols(c)],
            gb_send.at[c, d],
            gb_recv.at[c, d],
            at(g, rank),
        )

    def b_out(c):
        return Exchange(
            "exp",
            lambda t: zback.at[rows_at(t, zrows), bcols(c)],
            lambda s: bland.at[rows_at(s, zrows), bcols(c)],
            b_send.at[c],
            b_recv.at[c],
        )

    def second_layer(c):
        def one(r):
            return jnp.dot(hidden[r], wout_land[:, bcols(c)], preferred_element_type=F32)

        far_part[:, bcols(c)] = one(across).astype(BF16)
        go(far(c, 0))
        go(far(c, 1))
        product = one(above)
        up_part[second, bcols(c)] = product[mid:].astype(BF16)
        go(near(c, 0))
        up_wait[:, bcols(c)] = product[:mid]
        product = one(below)
        down_part[first, bcols(c)] = product[:mid].astype(BF16)
        go(near(c, 1))
        down_wait[:, bcols(c)] = product[mid:]
        own_part[:, bcols(c)] = one(rank)

    def add_far(c):
        far(c, 0).wait_recv()
        up_part[first, bcols(c)] = (
            up_wait[:, bcols(c)] + half_up[:, bcols(c)].astype(F32)
        ).astype(BF16)
        go(near(c, 2))
        far(c, 1).wait_recv()
        down_part[second, bcols(c)] = (
            down_wait[:, bcols(c)] + half_down[:, bcols(c)].astype(F32)
        ).astype(BF16)
        go(near(c, 3))

    def finish(c):
        for i in (0, 1, 2, 3):
            near(c, i).wait_recv()
        brows[:, bcols(c)] = (
            own_part[:, bcols(c)]
            + full_up[:, bcols(c)].astype(F32)
            + full_down[:, bcols(c)].astype(F32)
        ).astype(BF16)
        for d in range(1, experts):
            go(from_line(c, d, line))
        gback[rows_at(line, srows), bcols(c)] = brows[rows_at(line, srows), bcols(c)]

    def give_back(c):
        for d in range(1, experts):
            from_line(c, d, turn(line, -d)).wait_recv()
        zback[:, bcols(c)] = jnp.dot(
            inverse, gback[:, bcols(c)], preferred_element_type=F32
        ).astype(BF16)
        go(b_out(c))
        bland[rows_at(exp, zrows), bcols(c)] = zback[rows_at(exp, zrows), bcols(c)]

    second_layer(0)
    add_far(0)
    for c in range(1, back_chunks):
        second_layer(c)
        finish(c - 1)
        add_far(c)
        give_back(c - 1)
    finish(back_chunks - 1)
    give_back(back_chunks - 1)

    q_out = Exchange(
        "seq", lambda t: qsend.at[t], lambda s: qland.at[s], q_send, q_recv
    )
    go(q_out)
    qland[seq] = qsend[seq]

    diagonal = out_row == in_row
    gate = jnp.sum(jnp.where(diagonal, gate_ref[...], 0.0), axis=1, keepdims=True)
    for c in range(back_chunks):
        b_out(c).arrived()
        combined = lax.dot_general(
            place[...], bland[:, bcols(c)], (((0,), (0,)), ((), ())), preferred_element_type=F32
        )
        enc_out_ref[:, bcols(c)] = (enc[:, bcols(c)].astype(F32) + gate * combined).astype(BF16)
    block = rms_scale(enc_out_ref[...].astype(F32), final_gain_ref[...]).astype(BF16)
    for copy in projections:
        copy.wait()
    lane = lax.broadcasted_iota(jnp.int32, (tok, 128), 1)
    low = lane < 64
    for g in range(HEADS // 4):
        span = slice(g * 256, (g + 1) * 256)
        keys = jnp.dot(block, w_key[:, span], preferred_element_type=F32)
        values = jnp.dot(block, w_value[:, span], preferred_element_type=F32)
        for i in range(2):
            k_pair = pltpu.roll(keys[:, i * 128 : (i + 1) * 128], 64, 1)
            v_pair = values[:, i * 128 : (i + 1) * 128]
            head = g * 4 + i * 2
            kvsend[head] = jnp.where(low, v_pair, k_pair).astype(BF16)
            kvsend[head + 1] = jnp.where(low, k_pair, v_pair).astype(BF16)
    kv_out = Exchange(
        "seq",
        lambda t: kvsend.at[t],
        lambda s: kvland.at[rows_at(s, tok)],
        k_send,
        k_recv,
        route=lambda d: at(turn(line, d // experts), turn(rank, lax.rem(d, experts))),
    )
    per = n_seq // KEY_GROUPS
    kv_out.start(1, per)
    kvland[0:tok, :] = kvsend[seq]

    q_out.arrived()
    even = lax.rem(seq, 2) == 0
    q_count = 2 * q_half
    folded = qland[...].reshape(n_seq * q_half, 128).astype(F32)
    turned = pltpu.roll(folded, 64, 1)
    side = lax.broadcasted_iota(jnp.int32, folded.shape, 1)
    at_keys = jnp.where(even, side, side + 64) % 128 >= 64
    top = jnp.where(at_keys, jnp.where(even, turned, folded), 0.0).astype(BF16)
    bottom = jnp.where(at_keys, jnp.where(even, folded, turned), 0.0).astype(BF16)
    for t in range(n_seq):
        qrows[t * q_count : t * q_count + q_half, :] = top[t * q_half : (t + 1) * q_half]
        qrows[t * q_count + q_half : (t + 1) * q_count, :] = bottom[t * q_half : (t + 1) * q_half]

    kv_out.loop(kv_out.send_one, 1, per)
    kv_out.start(per, n_seq)
    c_out = Exchange("seq", lambda t: csend.at[t], lambda s: cland.at[s], c_send, c_recv)
    span_rows = kvland.shape[0] // KEY_GROUPS
    wide_lane = lax.broadcasted_iota(jnp.int32, (span_rows, 128), 1)
    is_key = jnp.where(even, wide_lane, wide_lane + 64) % 128 >= 64
    pair_rows = 2 * q_count
    lane = lax.broadcasted_iota(jnp.int32, (q_half, 128), 1)
    at_values = jnp.where(even, lane, lane + 64) % 128 < 64
    group = 4

    def attend(part, last):
        span = slice(part * span_rows, (part + 1) * span_rows)
        kv_out.arrived(max(1, part * per), (part + 1) * per)
        vland[span, :] = jnp.where(is_key, jnp.ones((), BF16), kvland[span, :])

        def step(d, carry):
            g = lax.rem(seq // group + d + 1, n_seq // group)
            tiles = [rows_at(2 * g + i, pair_rows) for i in range(2)]
            both = [
                lax.dot_general(
                    qrows[tile, :],
                    kvland[span, :],
                    (((1,), (1,)), ((), ())),
                    preferred_element_type=F32,
                )
                for tile in tiles
            ]
            for i, tile in enumerate(tiles):
                peak = jnp.max(both[i], axis=-1, keepdims=True)
                if part:
                    old = peaks[tile, 0:1]
                    peak = jnp.maximum(peak, old)
                expo = jnp.exp(both[i] - peak).astype(BF16)
                mixed = jnp.dot(expo, vland[span, :], preferred_element_type=F32)
                if part:
                    mixed = mixed + jnp.exp(old - peak) * sums[tile, :]
                if not last:
                    sums[tile, :] = mixed
                    peaks[tile, :] = jnp.broadcast_to(peak, mixed.shape)
                    continue
                context = mixed / pltpu.roll(mixed, 64, 1)
                turned = pltpu.roll(context, 64, 1)
                for j in range(2):
                    k = j * q_count
                    csend[g * group + 2 * i + j] = jnp.where(
                        at_values, context[k : k + q_half], turned[k + q_half : k + q_count]
                    ).astype(BF16)
            if last:
                for i in range(group):
                    t = g * group + i

                    @pl.when(t != seq)
                    def _():
                        c_out.start_one(lax.rem(t - seq + n_seq, n_seq))

            return carry

        lax.fori_loop(0, n_seq // group, step, 0)

    for part in range(KEY_GROUPS):
        attend(part, part == KEY_GROUPS - 1)
    started.append(c_out)
    cland[seq] = csend[seq]
    c_out.arrived()
    for p in range(HEADS // 2):
        one, two = cland[2 * p].astype(F32), cland[2 * p + 1].astype(F32)
        out_ref[:q_half, p * 128 : (p + 1) * 128] = jnp.where(lane < 64, one, two).astype(BF16)
        out_ref[q_half:, p * 128 : (p + 1) * 128] = pltpu.roll(
            jnp.where(lane < 64, two, one), 64, 1
        ).astype(BF16)
    kv_out.loop(kv_out.send_one, per, n_seq)
    for transfer in started:
        transfer.wait_send()


def per_device(
    enc_in,
    expert_ids,
    slots,
    expert_gate,
    moe_gain,
    w_in,
    w_out,
    final_gain,
    w_key,
    w_value,
    dec_query,
):
    n_exp, n_seq = lax.axis_size("exp"), lax.axis_size("seq")
    tok_rows, width = enc_in.shape[1:]
    experts, _, part_ff = w_in.shape
    q_rows = dec_query.shape[1]

    vmem = pl.BlockSpec(memory_space=pltpu.VMEM)
    hbm = pl.BlockSpec(memory_space=pl.ANY)
    dma = pltpu.SemaphoreType.DMA
    whole = pltpu.VMEM((tok_rows, width), BF16)
    half = pltpu.VMEM((tok_rows // 2, width), BF16)
    weight = pltpu.VMEM((experts * part_ff, width), BF16)
    square = pltpu.VMEM((width, width), BF16)
    folded = pltpu.VMEM((n_seq, q_rows // 2, 128), BF16)
    enc_out, context = pl.pallas_call(
        layer_kernel,
        out_shape=(
            jax.ShapeDtypeStruct((tok_rows, width), BF16),
            jax.ShapeDtypeStruct((q_rows, width), BF16),
        ),
        in_specs=[hbm, vmem, vmem, vmem, vmem, hbm, hbm, vmem, hbm, hbm, hbm],
        out_specs=(vmem, vmem),
        scratch_shapes=[
            whole,
            pltpu.VMEM((q_rows, width), BF16),
            pltpu.VMEM((tok_rows, tok_rows), BF16),
            square,
            square,
            whole,
            whole,
            whole,
            pltpu.VMEM((experts, tok_rows, width), BF16),
            weight,
            weight,
            pltpu.VMEM((experts, tok_rows, experts * part_ff), BF16),
            whole,
            whole,
            whole,
            pltpu.VMEM((tok_rows // 2, width), F32),
            pltpu.VMEM((tok_rows // 2, width), F32),
            pltpu.VMEM((tok_rows, width), F32),
            half,
            half,
            whole,
            whole,
            whole,
            whole,
            whole,
            whole,
            folded,
            folded,
            pltpu.VMEM((n_seq * q_rows, 128), BF16),
            pltpu.VMEM((n_seq, tok_rows, 128), BF16),
            pltpu.VMEM((n_seq * tok_rows, 128), BF16),
            pltpu.VMEM((n_seq * tok_rows, 128), BF16),
            pltpu.VMEM((n_seq * q_rows, 128), F32),
            pltpu.VMEM((n_seq * q_rows, 128), F32),
            folded,
            folded,
            dma((6,)),
        ]
        + [dma((OUT_CHUNKS, n_exp))] * 2
        + [dma((BACK_CHUNKS, n_exp))] * 2
        + [dma((n_seq,))] * 2
        + [dma((experts,))] * 4
        + [dma((OUT_CHUNKS, experts))] * 8
        + [dma((BACK_CHUNKS, 2))] * 2
        + [dma((BACK_CHUNKS, 4))] * 2
        + [dma((BACK_CHUNKS, experts))] * 2
        + [dma((n_seq,))] * 4,
        compiler_params=pltpu.CompilerParams(
            collective_id=0, has_side_effects=True, vmem_limit_bytes=56 << 20
        ),
        name="layer",
    )(
        enc_in[0],
        expert_ids,
        slots,
        expert_gate,
        moe_gain[None],
        jnp.swapaxes(w_in, 1, 2),
        w_out,
        final_gain[None],
        w_key,
        w_value,
        dec_query[0],
    )
    return (enc_out[None], context[None])


def solution(mesh):
    placed = (
        P("exp", "seq", None),
        P("exp", "seq"),
        P("exp", "seq"),
        P("exp", "seq"),
        P(),
        P("exp", None, "seq"),
        P("exp", "seq", None),
        P(),
        P(),
        P(),
        P("exp", "seq", None),
    )
    return jax.shard_map(
        per_device,
        mesh=mesh,
        in_specs=placed,
        out_specs=(P("exp", "seq", None), P("exp", "seq", None)),
        check_vma=False,
    )
```

```python
import functools

import jax
import jax.numpy as jnp
from jax import lax
from jax.experimental import pallas as pl
from jax.experimental.pallas import tpu as pltpu
from jax.sharding import PartitionSpec as P

HEADS = 16
OUT_CHUNKS = 1
BACK_CHUNKS = 2
KEY_GROUPS = 2
MESH = pl.DeviceIdType.MESH
F32 = jnp.float32
BF16 = jnp.bfloat16


def rms_scale(values, gain):
    mean_square = jnp.mean(values * values, axis=-1, keepdims=True)
    return values * lax.rsqrt(mean_square + 1e-06) * gain


def rows_at(index, count):
    return pl.ds(pl.multiple_of(index * count, count), count)


def signal_all(axes):
    barrier = pltpu.get_barrier_semaphore()
    total = 0
    for axis in axes:
        n = lax.axis_size(axis)
        me = lax.axis_index(axis)
        total += n - 1

        def signal(d, carry, axis=axis, n=n, me=me):
            pl.semaphore_signal(
                barrier, inc=1, device_id={axis: lax.rem(me + d, n)}, device_id_type=MESH
            )
            return carry

        lax.fori_loop(1, n, signal, 0)
    return barrier, total


class Exchange:
    def __init__(self, axis, source, landing, send, recv, route=None):
        self.route, self.by_step = route, route is not None
        self.axis, self.source, self.landing = axis, source, landing
        self.send, self.recv = send, recv
        self.n, self.me = lax.axis_size(axis), lax.axis_index(axis)

    def copy(self, d, slot):
        t = self.route(d) if self.route else lax.rem(self.me + d, self.n)
        return pltpu.make_async_remote_copy(
            src_ref=self.source(t),
            dst_ref=self.landing(slot),
            send_sem=self.send.at[d],
            recv_sem=self.recv.at[d],
            device_id={self.axis: t},
            device_id_type=MESH,
        )

    def start_one(self, d):
        self.copy(d, d if self.by_step else self.me).start()

    def wait_one(self, d):
        slot = d if self.by_step else lax.rem(self.me + self.n - d, self.n)
        self.copy(d, slot).wait_recv()

    def loop(self, act, first=1, last=None):
        def body(d, carry):
            act(d)
            return carry

        lax.fori_loop(first, self.n if last is None else last, body, 0)

    def start(self, first=1, last=None):
        self.loop(self.start_one, first, last)

    def arrived(self, first=1, last=None):
        self.loop(self.wait_one, first, last)

    def send_one(self, d):
        self.copy(d, self.me).wait_send()

    def wait_send(self):
        self.loop(lambda d: self.copy(d, self.me).wait_send())


def remote(src, dst, send, recv, seq):
    return pltpu.make_async_remote_copy(
        src_ref=src,
        dst_ref=dst,
        send_sem=send,
        recv_sem=recv,
        device_id={"seq": seq},
        device_id_type=MESH,
    )


def layer_kernel(
    enc_ref,
    ids_ref,
    slots_ref,
    gate_ref,
    gain_ref,
    win_ref,
    wout_ref,
    final_gain_ref,
    wk_ref,
    wv_ref,
    q_ref,
    enc_out_ref,
    out_ref,
    enc,
    query,
    place,
    w_key,
    w_value,
    packed,
    zland,
    rows,
    rland,
    win_land,
    wout_land,
    hidden,
    far_part,
    up_part,
    down_part,
    up_wait,
    down_wait,
    own_part,
    half_up,
    half_down,
    full_up,
    full_down,
    brows,
    gback,
    zback,
    bland,
    qsend,
    qland,
    qrows,
    kvsend,
    kvland,
    vland,
    sums,
    peaks,
    csend,
    cland,
    local_sem,
    z_send,
    z_recv,
    b_send,
    b_recv,
    q_send,
    q_recv,
    wi_send,
    wi_recv,
    wo_send,
    wo_recv,
    g_send,
    g_recv,
    up_send,
    up_recv,
    down_send,
    down_recv,
    fwd_send,
    fwd_recv,
    h_send,
    h_recv,
    f_send,
    f_recv,
    gb_send,
    gb_recv,
    k_send,
    k_recv,
    c_send,
    c_recv,
):
    seq, exp = lax.axis_index("seq"), lax.axis_index("exp")
    n_seq, n_exp = lax.axis_size("seq"), lax.axis_size("exp")
    experts = win_ref.shape[0]
    hidden_part = win_ref.shape[1]
    tok = enc_ref.shape[0]
    zrows, srows = tok // n_exp, tok // experts
    capacity = zrows // experts
    core = lax.rem(exp, 2)
    y, x = seq // experts, lax.rem(seq, experts)
    line, rank = y + core * (x - y), x + core * (y - x)

    def at(g, r):
        return g * (experts - core * (experts - 1)) + r * (1 + core * (experts - 1))

    def turn(value, d):
        return lax.rem(value + experts + d, experts)

    enc_in = pltpu.make_async_copy(enc_ref, enc, local_sem.at[0])
    q_in = pltpu.make_async_copy(q_ref, query, local_sem.at[1])
    enc_in.start()
    q_in.start()
    barrier, greeted = signal_all(("seq", "exp"))
    projections = [
        pltpu.make_async_copy(ref, land, local_sem.at[4 + i])
        for i, (ref, land) in enumerate(((wk_ref, w_key), (wv_ref, w_value)))
    ]
    own_weights = [
        pltpu.make_async_copy(
            ref.at[line], land.at[rows_at(line, hidden_part)], local_sem.at[2 + i]
        )
        for i, (ref, land) in enumerate(((win_ref, win_land), (wout_ref, wout_land)))
    ]
    for copy in own_weights:
        copy.start()
    enc_in.wait()
    normed = rms_scale(enc[...].astype(F32), gain_ref[...]).astype(BF16)
    target = jnp.where(slots_ref[...] < capacity, ids_ref[...] * capacity + slots_ref[...], -1)
    out_row = lax.broadcasted_iota(jnp.int32, (tok, tok), 0)
    in_row = lax.broadcasted_iota(jnp.int32, (tok, tok), 1)
    place[...] = (out_row == target).astype(BF16)
    packed[...] = jnp.dot(place[...], normed, preferred_element_type=F32).astype(BF16)
    q_in.wait()
    q_half = q_ref.shape[0] // 2
    lane = lax.broadcasted_iota(jnp.int32, (q_half, 128), 1)
    for p in range(HEADS // 2):
        pair = query[:, p * 128 : (p + 1) * 128].astype(F32) * 0.125
        turned = pltpu.roll(pair, 64, 1)
        qsend[2 * p] = jnp.where(lane < 64, pair[:q_half], turned[q_half:]).astype(BF16)
        qsend[2 * p + 1] = jnp.where(lane < 64, turned[:q_half], pair[q_half:]).astype(BF16)
    pl.semaphore_wait(barrier, greeted)

    started, late = [], []

    def go(transfer, group=started):
        transfer.start()
        group.append(transfer)

    def drain(group):
        for transfer in group:
            transfer.wait_send()

    chunks, back_chunks = z_send.shape[0], b_send.shape[0]
    wide = enc_ref.shape[1] // chunks
    back_wide = enc_ref.shape[1] // back_chunks

    def cols(c):
        return pl.ds(c * wide, wide)

    def bcols(c):
        return pl.ds(c * back_wide, back_wide)

    def z_out(c):
        return Exchange(
            "exp",
            lambda t: packed.at[rows_at(t, zrows), cols(c)],
            lambda s: zland.at[rows_at(s, zrows), cols(c)],
            z_send.at[c],
            z_recv.at[c],
        )

    def weight_copy(d, slot, ref, land, send, recv):
        k = turn(line, d)
        return remote(
            ref.at[k], land.at[rows_at(slot, hidden_part)], send.at[d], recv.at[d], at(k, rank)
        )

    w_first = (win_ref, win_land, wi_send, wi_recv)
    w_second = (wout_ref, wout_land, wo_send, wo_recv)
    direct = [(d, w_first) for d in range(1, experts)] + [(d, w_second) for d in range(1, experts)]
    go(z_out(0))
    for d, each in direct:
        go(weight_copy(d, line, *each))
    for c in range(1, chunks):
        go(z_out(c))
    for copy in projections:
        copy.start()
    zland[rows_at(exp, zrows), :] = packed[rows_at(exp, zrows), :]

    def by_expert(r):
        j, k, c = r // zrows, lax.rem(r // capacity, experts), lax.rem(r, capacity)
        return k * srows + j * capacity + c

    forward = (by_expert(in_row) == out_row).astype(BF16)
    inverse = (by_expert(out_row) == in_row).astype(BF16)

    above, below, across = turn(rank, 1), turn(rank, -1), turn(rank, 2)

    def piece(r, g, c):
        return rland.at[r, rows_at(g, srows), cols(c)]

    def to_line(c, d, slot):
        k = turn(line, d)
        return remote(
            rows.at[rows_at(k, srows), cols(c)],
            piece(rank, slot, c),
            g_send.at[c, d],
            g_recv.at[c, d],
            at(k, rank),
        )

    def up(c, d, r):
        g = turn(line, -d)
        return remote(
            piece(rank, g, c), piece(r, g, c), up_send.at[c, d], up_recv.at[c, d], at(line, above)
        )

    def down(c, d, r):
        g = turn(line, -d)
        return remote(
            piece(rank, g, c),
            piece(r, g, c),
            down_send.at[c, d],
            down_recv.at[c, d],
            at(line, below),
        )

    def forwarded(c, d, r):
        g = turn(line, -d)
        way = 1 if d < 2 else -1
        return remote(
            piece(turn(rank, -way), g, c),
            piece(r, g, c),
            fwd_send.at[c, d],
            fwd_recv.at[c, d],
            at(line, turn(rank, way)),
        )

    for c in range(chunks):
        z_out(c).arrived()
        rows[:, cols(c)] = jnp.dot(
            forward, zland[:, cols(c)], preferred_element_type=F32
        ).astype(BF16)
        for d in range(1, experts):
            go(to_line(c, d, line))
        rland[rank, rows_at(line, srows), cols(c)] = rows[rows_at(line, srows), cols(c)]
        for d in range(experts):
            if d:
                to_line(c, d, turn(line, -d)).wait_recv()
            go(up(c, d, rank))
            go(down(c, d, rank))
        for d in (0, 1):
            up(c, d, below).wait_recv()
            go(forwarded(c, d, below))
        for d in (2, 3):
            down(c, d, above).wait_recv()
            go(forwarded(c, d, above))

    def first_layer(r):
        product = lax.dot_general(
            rland[r], win_land[...], (((1,), (1,)), ((), ())), preferred_element_type=F32
        )
        hidden[r] = jnp.maximum(product, 0.0).astype(BF16)

    for copy in own_weights:
        copy.wait()
    for d, each in direct:
        if each is w_first:
            weight_copy(d, turn(line, -d), *each).wait_recv()
    first_layer(rank)
    for c in range(chunks):
        for d in (2, 3):
            up(c, d, below).wait_recv()
    first_layer(below)
    for c in range(chunks):
        for d in (0, 1):
            down(c, d, above).wait_recv()
    first_layer(above)
    for c in range(chunks):
        for d in range(experts):
            forwarded(c, d, across).wait_recv()
    first_layer(across)
    for d, each in direct:
        if each is w_second:
            weight_copy(d, turn(line, -d), *each).wait_recv()

    mid = tok // 2
    first, second = pl.ds(0, mid), pl.ds(mid, mid)

    def far(c, way):
        half, land, r = ((first, half_up, above), (second, half_down, below))[way]
        return remote(
            far_part.at[half, bcols(c)],
            land.at[:, bcols(c)],
            h_send.at[c, way],
            h_recv.at[c, way],
            at(line, r),
        )

    def near(c, i):
        r, half, source, land = (
            (above, second, up_part, full_up),
            (below, first, down_part, full_down),
            (above, first, up_part, full_up),
            (below, second, down_part, full_down),
        )[i]
        return remote(
            source.at[half, bcols(c)],
            land.at[half, bcols(c)],
            f_send.at[c, i],
            f_recv.at[c, i],
            at(line, r),
        )

    def from_line(c, d, slot):
        g = turn(line, d)
        return remote(
            brows.at[rows_at(g, srows), bcols(c)],
            gback.at[rows_at(slot, srows), bcols(c)],
            gb_send.at[c, d],
            gb_recv.at[c, d],
            at(g, rank),
        )

    def b_out(c):
        return Exchange(
            "exp",
            lambda t: zback.at[rows_at(t, zrows), bcols(c)],
            lambda s: bland.at[rows_at(s, zrows), bcols(c)],
            b_send.at[c],
            b_recv.at[c],
        )

    def second_layer(c):
        def one(r):
            return jnp.dot(hidden[r], wout_land[:, bcols(c)], preferred_element_type=F32)

        far_part[:, bcols(c)] = one(across).astype(BF16)
        go(far(c, 0))
        go(far(c, 1))
        product = one(above)
        up_part[second, bcols(c)] = product[mid:].astype(BF16)
        go(near(c, 0))
        up_wait[:, bcols(c)] = product[:mid]
        product = one(below)
        down_part[first, bcols(c)] = product[:mid].astype(BF16)
        go(near(c, 1))
        down_wait[:, bcols(c)] = product[mid:]
        own_part[:, bcols(c)] = one(rank)

    def add_far(c):
        far(c, 0).wait_recv()
        up_part[first, bcols(c)] = (
            up_wait[:, bcols(c)] + half_up[:, bcols(c)].astype(F32)
        ).astype(BF16)
        go(near(c, 2))
        far(c, 1).wait_recv()
        down_part[second, bcols(c)] = (
            down_wait[:, bcols(c)] + half_down[:, bcols(c)].astype(F32)
        ).astype(BF16)
        go(near(c, 3))

    def finish(c):
        for i in (0, 1, 2, 3):
            near(c, i).wait_recv()
        brows[:, bcols(c)] = (
            own_part[:, bcols(c)]
            + full_up[:, bcols(c)].astype(F32)
            + full_down[:, bcols(c)].astype(F32)
        ).astype(BF16)
        for d in range(1, experts):
            go(from_line(c, d, line))
        gback[rows_at(line, srows), bcols(c)] = brows[rows_at(line, srows), bcols(c)]

    def give_back(c):
        for d in range(1, experts):
            from_line(c, d, turn(line, -d)).wait_recv()
        zback[:, bcols(c)] = jnp.dot(
            inverse, gback[:, bcols(c)], preferred_element_type=F32
        ).astype(BF16)
        go(b_out(c), late)
        bland[rows_at(exp, zrows), bcols(c)] = zback[rows_at(exp, zrows), bcols(c)]

    second_layer(0)
    add_far(0)
    for c in range(1, back_chunks):
        second_layer(c)
        finish(c - 1)
        add_far(c)
        give_back(c - 1)
    finish(back_chunks - 1)
    give_back(back_chunks - 1)

    q_out = Exchange(
        "seq", lambda t: qsend.at[t], lambda s: qland.at[s], q_send, q_recv
    )
    go(q_out, late)
    qland[seq] = qsend[seq]

    drain(started)
    diagonal = out_row == in_row
    gate = jnp.sum(jnp.where(diagonal, gate_ref[...], 0.0), axis=1, keepdims=True)
    for c in range(back_chunks):
        b_out(c).arrived()
        combined = lax.dot_general(
            place[...], bland[:, bcols(c)], (((0,), (0,)), ((), ())), preferred_element_type=F32
        )
        enc_out_ref[:, bcols(c)] = (enc[:, bcols(c)].astype(F32) + gate * combined).astype(BF16)
    block = rms_scale(enc_out_ref[...].astype(F32), final_gain_ref[...]).astype(BF16)
    for copy in projections:
        copy.wait()
    lane = lax.broadcasted_iota(jnp.int32, (tok, 128), 1)
    low = lane < 64
    for g in range(HEADS // 4):
        span = slice(g * 256, (g + 1) * 256)
        keys = jnp.dot(block, w_key[:, span], preferred_element_type=F32)
        values = jnp.dot(block, w_value[:, span], preferred_element_type=F32)
        for i in range(2):
            k_pair = pltpu.roll(keys[:, i * 128 : (i + 1) * 128], 64, 1)
            v_pair = values[:, i * 128 : (i + 1) * 128]
            head = g * 4 + i * 2
            kvsend[head] = jnp.where(low, v_pair, k_pair).astype(BF16)
            kvsend[head + 1] = jnp.where(low, k_pair, v_pair).astype(BF16)
    kv_out = Exchange(
        "seq",
        lambda t: kvsend.at[t],
        lambda s: kvland.at[rows_at(s, tok)],
        k_send,
        k_recv,
        route=lambda d: at(turn(line, d // experts), turn(rank, lax.rem(d, experts))),
    )
    per = n_seq // KEY_GROUPS
    kv_out.start(1, per)
    kvland[0:tok, :] = kvsend[seq]

    q_out.arrived()
    even = lax.rem(seq, 2) == 0
    q_count = 2 * q_half
    folded = qland[...].reshape(n_seq * q_half, 128).astype(F32)
    turned = pltpu.roll(folded, 64, 1)
    side = lax.broadcasted_iota(jnp.int32, folded.shape, 1)
    at_keys = jnp.where(even, side, side + 64) % 128 >= 64
    top = jnp.where(at_keys, jnp.where(even, turned, folded), 0.0).astype(BF16)
    bottom = jnp.where(at_keys, jnp.where(even, folded, turned), 0.0).astype(BF16)
    for t in range(n_seq):
        qrows[t * q_count : t * q_count + q_half, :] = top[t * q_half : (t + 1) * q_half]
        qrows[t * q_count + q_half : (t + 1) * q_count, :] = bottom[t * q_half : (t + 1) * q_half]

    drain(late)
    kv_out.loop(kv_out.send_one, 1, per)
    kv_out.start(per, n_seq)
    c_out = Exchange("seq", lambda t: csend.at[t], lambda s: cland.at[s], c_send, c_recv)
    span_rows = kvland.shape[0] // KEY_GROUPS
    wide_lane = lax.broadcasted_iota(jnp.int32, (span_rows, 128), 1)
    is_key = jnp.where(even, wide_lane, wide_lane + 64) % 128 >= 64
    pair_rows = 2 * q_count
    lane = lax.broadcasted_iota(jnp.int32, (q_half, 128), 1)
    at_values = jnp.where(even, lane, lane + 64) % 128 < 64
    group = 4

    def attend(part, last):
        span = slice(part * span_rows, (part + 1) * span_rows)
        kv_out.arrived(max(1, part * per), (part + 1) * per)
        if last:
            kv_out.loop(kv_out.send_one, per, n_seq)
        vland[span, :] = jnp.where(is_key, jnp.ones((), BF16), kvland[span, :])

        def step(d, carry):
            g = lax.rem(seq // group + d + 1, n_seq // group)
            tiles = [rows_at(2 * g + i, pair_rows) for i in range(2)]
            both = [
                lax.dot_general(
                    qrows[tile, :],
                    kvland[span, :],
                    (((1,), (1,)), ((), ())),
                    preferred_element_type=F32,
                )
                for tile in tiles
            ]
            for i, tile in enumerate(tiles):
                peak = jnp.max(both[i], axis=-1, keepdims=True)
                if part:
                    old = peaks[tile, 0:1]
                    peak = jnp.maximum(peak, old)
                expo = jnp.exp(both[i] - peak).astype(BF16)
                mixed = jnp.dot(expo, vland[span, :], preferred_element_type=F32)
                if part:
                    mixed = mixed + jnp.exp(old - peak) * sums[tile, :]
                if not last:
                    sums[tile, :] = mixed
                    peaks[tile, :] = jnp.broadcast_to(peak, mixed.shape)
                    continue
                context = mixed / pltpu.roll(mixed, 64, 1)
                turned = pltpu.roll(context, 64, 1)
                for j in range(2):
                    k = j * q_count
                    csend[g * group + 2 * i + j] = jnp.where(
                        at_values, context[k : k + q_half], turned[k + q_half : k + q_count]
                    ).astype(BF16)
            if last:
                for i in range(group):
                    t = g * group + i

                    @pl.when(t != seq)
                    def _():
                        c_out.start_one(lax.rem(t - seq + n_seq, n_seq))

            return carry

        lax.fori_loop(0, n_seq // group, step, 0, unroll=2)

    for part in range(KEY_GROUPS):
        attend(part, part == KEY_GROUPS - 1)
    cland[seq] = csend[seq]
    c_out.arrived()
    for p in range(HEADS // 2):
        one, two = cland[2 * p].astype(F32), cland[2 * p + 1].astype(F32)
        out_ref[:q_half, p * 128 : (p + 1) * 128] = jnp.where(lane < 64, one, two).astype(BF16)
        out_ref[q_half:, p * 128 : (p + 1) * 128] = pltpu.roll(
            jnp.where(lane < 64, two, one), 64, 1
        ).astype(BF16)
    c_out.wait_send()


def per_device(
    enc_in,
    expert_ids,
    slots,
    expert_gate,
    moe_gain,
    w_in,
    w_out,
    final_gain,
    w_key,
    w_value,
    dec_query,
):
    n_exp, n_seq = lax.axis_size("exp"), lax.axis_size("seq")
    tok_rows, width = enc_in.shape[1:]
    experts, _, part_ff = w_in.shape
    q_rows = dec_query.shape[1]

    vmem = pl.BlockSpec(memory_space=pltpu.VMEM)
    hbm = pl.BlockSpec(memory_space=pl.ANY)
    dma = pltpu.SemaphoreType.DMA
    whole = pltpu.VMEM((tok_rows, width), BF16)
    half = pltpu.VMEM((tok_rows // 2, width), BF16)
    weight = pltpu.VMEM((experts * part_ff, width), BF16)
    square = pltpu.VMEM((width, width), BF16)
    folded = pltpu.VMEM((n_seq, q_rows // 2, 128), BF16)
    enc_out, context = pl.pallas_call(
        layer_kernel,
        out_shape=(
            jax.ShapeDtypeStruct((tok_rows, width), BF16),
            jax.ShapeDtypeStruct((q_rows, width), BF16),
        ),
        in_specs=[hbm, vmem, vmem, vmem, vmem, hbm, hbm, vmem, hbm, hbm, hbm],
        out_specs=(vmem, vmem),
        scratch_shapes=[
            whole,
            pltpu.VMEM((q_rows, width), BF16),
            pltpu.VMEM((tok_rows, tok_rows), BF16),
            square,
            square,
            whole,
            whole,
            whole,
            pltpu.VMEM((experts, tok_rows, width), BF16),
            weight,
            weight,
            pltpu.VMEM((experts, tok_rows, experts * part_ff), BF16),
            whole,
            whole,
            whole,
            pltpu.VMEM((tok_rows // 2, width), F32),
            pltpu.VMEM((tok_rows // 2, width), F32),
            pltpu.VMEM((tok_rows, width), F32),
            half,
            half,
            whole,
            whole,
            whole,
            whole,
            whole,
            whole,
            folded,
            folded,
            pltpu.VMEM((n_seq * q_rows, 128), BF16),
            pltpu.VMEM((n_seq, tok_rows, 128), BF16),
            pltpu.VMEM((n_seq * tok_rows, 128), BF16),
            pltpu.VMEM((n_seq * tok_rows, 128), BF16),
            pltpu.VMEM((n_seq * q_rows, 128), F32),
            pltpu.VMEM((n_seq * q_rows, 128), F32),
            folded,
            folded,
            dma((6,)),
        ]
        + [dma((OUT_CHUNKS, n_exp))] * 2
        + [dma((BACK_CHUNKS, n_exp))] * 2
        + [dma((n_seq,))] * 2
        + [dma((experts,))] * 4
        + [dma((OUT_CHUNKS, experts))] * 8
        + [dma((BACK_CHUNKS, 2))] * 2
        + [dma((BACK_CHUNKS, 4))] * 2
        + [dma((BACK_CHUNKS, experts))] * 2
        + [dma((n_seq,))] * 4,
        compiler_params=pltpu.CompilerParams(
            collective_id=0, has_side_effects=True, vmem_limit_bytes=56 << 20
        ),
        name="layer",
    )(
        enc_in[0],
        expert_ids,
        slots,
        expert_gate,
        moe_gain[None],
        jnp.swapaxes(w_in, 1, 2),
        w_out,
        final_gain[None],
        w_key,
        w_value,
        dec_query[0],
    )
    return (enc_out[None], context[None])


def solution(mesh):
    placed = (
        P("exp", "seq", None),
        P("exp", "seq"),
        P("exp", "seq"),
        P("exp", "seq"),
        P(),
        P("exp", None, "seq"),
        P("exp", "seq", None),
        P(),
        P(),
        P(),
        P("exp", "seq", None),
    )
    return jax.shard_map(
        per_device,
        mesh=mesh,
        in_specs=placed,
        out_specs=(P("exp", "seq", None), P("exp", "seq", None)),
        check_vma=False,
    )
```

```python
import functools

import jax
import jax.numpy as jnp
from jax import lax
from jax.experimental import pallas as pl
from jax.experimental.pallas import tpu as pltpu
from jax.sharding import PartitionSpec as P

HEADS = 16
OUT_CHUNKS = 1
BACK_CHUNKS = 2
KEY_GROUPS = 2
MESH = pl.DeviceIdType.MESH
F32 = jnp.float32
BF16 = jnp.bfloat16


def rms_scale(values, gain):
    mean_square = jnp.mean(values * values, axis=-1, keepdims=True)
    return values * lax.rsqrt(mean_square + 1e-06) * gain


def rows_at(index, count):
    return pl.ds(pl.multiple_of(index * count, count), count)


def signal_all(axes):
    barrier = pltpu.get_barrier_semaphore()
    total = 0
    for axis in axes:
        n = lax.axis_size(axis)
        me = lax.axis_index(axis)
        total += n - 1

        def signal(d, carry, axis=axis, n=n, me=me):
            pl.semaphore_signal(
                barrier, inc=1, device_id={axis: lax.rem(me + d, n)}, device_id_type=MESH
            )
            return carry

        lax.fori_loop(1, n, signal, 0)
    return barrier, total


class Exchange:
    def __init__(self, axis, source, landing, send, recv, route=None):
        self.route, self.by_step = route, route is not None
        self.axis, self.source, self.landing = axis, source, landing
        self.send, self.recv = send, recv
        self.n, self.me = lax.axis_size(axis), lax.axis_index(axis)

    def copy(self, d, slot):
        t = self.route(d) if self.route else lax.rem(self.me + d, self.n)
        return pltpu.make_async_remote_copy(
            src_ref=self.source(t),
            dst_ref=self.landing(slot),
            send_sem=self.send.at[d],
            recv_sem=self.recv.at[d],
            device_id={self.axis: t},
            device_id_type=MESH,
        )

    def start_one(self, d):
        self.copy(d, d if self.by_step else self.me).start()

    def wait_one(self, d):
        slot = d if self.by_step else lax.rem(self.me + self.n - d, self.n)
        self.copy(d, slot).wait_recv()

    def loop(self, act, first=1, last=None):
        def body(d, carry):
            act(d)
            return carry

        lax.fori_loop(first, self.n if last is None else last, body, 0)

    def start(self, first=1, last=None):
        if self.route:
            self.loop(self.start_one, first, last)
            return

        def outward(i):
            side = 2 * lax.rem(i, 2) - 1
            self.start_one(self.n // 2 + side * ((i + 1) // 2))

        self.loop(outward, 0, self.n - 1)

    def arrived(self, first=1, last=None):
        self.loop(self.wait_one, first, last)

    def send_one(self, d):
        self.copy(d, self.me).wait_send()

    def wait_send(self):
        self.loop(lambda d: self.copy(d, self.me).wait_send())


def remote(src, dst, send, recv, seq):
    return pltpu.make_async_remote_copy(
        src_ref=src,
        dst_ref=dst,
        send_sem=send,
        recv_sem=recv,
        device_id={"seq": seq},
        device_id_type=MESH,
    )


def layer_kernel(
    enc_ref,
    ids_ref,
    slots_ref,
    gate_ref,
    gain_ref,
    win_ref,
    wout_ref,
    final_gain_ref,
    wk_ref,
    wv_ref,
    q_ref,
    enc_out_ref,
    out_ref,
    enc,
    query,
    place,
    w_key,
    w_value,
    packed,
    zland,
    rows,
    rland,
    win_land,
    wout_land,
    hidden,
    far_part,
    up_part,
    down_part,
    up_wait,
    down_wait,
    own_part,
    half_up,
    half_down,
    full_up,
    full_down,
    brows,
    gback,
    zback,
    bland,
    qsend,
    qland,
    qrows,
    kvsend,
    kvland,
    vland,
    sums,
    peaks,
    csend,
    cland,
    local_sem,
    z_send,
    z_recv,
    b_send,
    b_recv,
    q_send,
    q_recv,
    wi_send,
    wi_recv,
    wo_send,
    wo_recv,
    g_send,
    g_recv,
    up_send,
    up_recv,
    down_send,
    down_recv,
    fwd_send,
    fwd_recv,
    h_send,
    h_recv,
    f_send,
    f_recv,
    gb_send,
    gb_recv,
    k_send,
    k_recv,
    c_send,
    c_recv,
):
    seq, exp = lax.axis_index("seq"), lax.axis_index("exp")
    n_seq, n_exp = lax.axis_size("seq"), lax.axis_size("exp")
    experts = win_ref.shape[0]
    hidden_part = win_ref.shape[1]
    tok = enc_ref.shape[0]
    zrows, srows = tok // n_exp, tok // experts
    capacity = zrows // experts
    core = lax.rem(exp, 2)
    y, x = seq // experts, lax.rem(seq, experts)
    line, rank = y + core * (x - y), x + core * (y - x)

    def at(g, r):
        return g * (experts - core * (experts - 1)) + r * (1 + core * (experts - 1))

    def turn(value, d):
        return lax.rem(value + experts + d, experts)

    enc_in = pltpu.make_async_copy(enc_ref, enc, local_sem.at[0])
    q_in = pltpu.make_async_copy(q_ref, query, local_sem.at[1])
    enc_in.start()
    q_in.start()
    barrier, greeted = signal_all(("seq", "exp"))
    projections = [
        pltpu.make_async_copy(ref, land, local_sem.at[4 + i])
        for i, (ref, land) in enumerate(((wk_ref, w_key), (wv_ref, w_value)))
    ]
    own_weights = [
        pltpu.make_async_copy(
            ref.at[line], land.at[rows_at(line, hidden_part)], local_sem.at[2 + i]
        )
        for i, (ref, land) in enumerate(((win_ref, win_land), (wout_ref, wout_land)))
    ]
    for copy in own_weights:
        copy.start()
    enc_in.wait()
    normed = rms_scale(enc[...].astype(F32), gain_ref[...]).astype(BF16)
    target = jnp.where(slots_ref[...] < capacity, ids_ref[...] * capacity + slots_ref[...], -1)
    out_row = lax.broadcasted_iota(jnp.int32, (tok, tok), 0)
    in_row = lax.broadcasted_iota(jnp.int32, (tok, tok), 1)
    place[...] = (out_row == target).astype(BF16)
    packed[...] = jnp.dot(place[...], normed, preferred_element_type=F32).astype(BF16)
    q_in.wait()
    q_half = q_ref.shape[0] // 2
    lane = lax.broadcasted_iota(jnp.int32, (q_half, 128), 1)
    for p in range(HEADS // 2):
        pair = query[:, p * 128 : (p + 1) * 128].astype(F32) * 0.125
        turned = pltpu.roll(pair, 64, 1)
        qsend[2 * p] = jnp.where(lane < 64, pair[:q_half], turned[q_half:]).astype(BF16)
        qsend[2 * p + 1] = jnp.where(lane < 64, turned[:q_half], pair[q_half:]).astype(BF16)
    pl.semaphore_wait(barrier, greeted)

    started, late = [], []

    def go(transfer, group=started):
        transfer.start()
        group.append(transfer)

    def drain(group):
        for transfer in group:
            transfer.wait_send()

    chunks, back_chunks = z_send.shape[0], b_send.shape[0]
    wide = enc_ref.shape[1] // chunks
    back_wide = enc_ref.shape[1] // back_chunks

    def cols(c):
        return pl.ds(c * wide, wide)

    def bcols(c):
        return pl.ds(c * back_wide, back_wide)

    def z_out(c):
        return Exchange(
            "exp",
            lambda t: packed.at[rows_at(t, zrows), cols(c)],
            lambda s: zland.at[rows_at(s, zrows), cols(c)],
            z_send.at[c],
            z_recv.at[c],
        )

    def weight_copy(d, slot, ref, land, send, recv):
        k = turn(line, d)
        return remote(
            ref.at[k], land.at[rows_at(slot, hidden_part)], send.at[d], recv.at[d], at(k, rank)
        )

    w_first = (win_ref, win_land, wi_send, wi_recv)
    w_second = (wout_ref, wout_land, wo_send, wo_recv)
    direct = [(d, w_first) for d in range(1, experts)] + [(d, w_second) for d in range(1, experts)]
    go(z_out(0))
    for d, each in direct:
        go(weight_copy(d, line, *each))
    for c in range(1, chunks):
        go(z_out(c))
    for copy in projections:
        copy.start()
    zland[rows_at(exp, zrows), :] = packed[rows_at(exp, zrows), :]

    def by_expert(r):
        j, k, c = r // zrows, lax.rem(r // capacity, experts), lax.rem(r, capacity)
        return k * srows + j * capacity + c

    forward = (by_expert(in_row) == out_row).astype(BF16)
    inverse = (by_expert(out_row) == in_row).astype(BF16)

    above, below, across = turn(rank, 1), turn(rank, -1), turn(rank, 2)

    def piece(r, g, c):
        return rland.at[r, rows_at(g, srows), cols(c)]

    def to_line(c, d, slot):
        k = turn(line, d)
        return remote(
            rows.at[rows_at(k, srows), cols(c)],
            piece(rank, slot, c),
            g_send.at[c, d],
            g_recv.at[c, d],
            at(k, rank),
        )

    def up(c, d, r):
        g = turn(line, -d)
        return remote(
            piece(rank, g, c), piece(r, g, c), up_send.at[c, d], up_recv.at[c, d], at(line, above)
        )

    def down(c, d, r):
        g = turn(line, -d)
        return remote(
            piece(rank, g, c),
            piece(r, g, c),
            down_send.at[c, d],
            down_recv.at[c, d],
            at(line, below),
        )

    def forwarded(c, d, r):
        g = turn(line, -d)
        way = 1 if d < 2 else -1
        return remote(
            piece(turn(rank, -way), g, c),
            piece(r, g, c),
            fwd_send.at[c, d],
            fwd_recv.at[c, d],
            at(line, turn(rank, way)),
        )

    for c in range(chunks):
        z_out(c).arrived()
        rows[:, cols(c)] = jnp.dot(
            forward, zland[:, cols(c)], preferred_element_type=F32
        ).astype(BF16)
        for d in range(1, experts):
            go(to_line(c, d, line))
        rland[rank, rows_at(line, srows), cols(c)] = rows[rows_at(line, srows), cols(c)]
        for d in range(experts):
            if d:
                to_line(c, d, turn(line, -d)).wait_recv()
            go(up(c, d, rank))
            go(down(c, d, rank))
        for d in (0, 1):
            up(c, d, below).wait_recv()
            go(forwarded(c, d, below))
        for d in (2, 3):
            down(c, d, above).wait_recv()
            go(forwarded(c, d, above))

    def first_layer(r):
        product = lax.dot_general(
            rland[r], win_land[...], (((1,), (1,)), ((), ())), preferred_element_type=F32
        )
        hidden[r] = jnp.maximum(product, 0.0).astype(BF16)

    for copy in own_weights:
        copy.wait()
    for d, each in direct:
        if each is w_first:
            weight_copy(d, turn(line, -d), *each).wait_recv()
    first_layer(rank)
    for c in range(chunks):
        for d in (2, 3):
            up(c, d, below).wait_recv()
    first_layer(below)
    for c in range(chunks):
        for d in (0, 1):
            down(c, d, above).wait_recv()
    first_layer(above)
    for c in range(chunks):
        for d in range(experts):
            forwarded(c, d, across).wait_recv()
    first_layer(across)
    for d, each in direct:
        if each is w_second:
            weight_copy(d, turn(line, -d), *each).wait_recv()

    mid = tok // 2
    first, second = pl.ds(0, mid), pl.ds(mid, mid)

    def far(c, way):
        half, land, r = ((first, half_up, above), (second, half_down, below))[way]
        return remote(
            far_part.at[half, bcols(c)],
            land.at[:, bcols(c)],
            h_send.at[c, way],
            h_recv.at[c, way],
            at(line, r),
        )

    def near(c, i):
        r, half, source, land = (
            (above, second, up_part, full_up),
            (below, first, down_part, full_down),
            (above, first, up_part, full_up),
            (below, second, down_part, full_down),
        )[i]
        return remote(
            source.at[half, bcols(c)],
            land.at[half, bcols(c)],
            f_send.at[c, i],
            f_recv.at[c, i],
            at(line, r),
        )

    def from_line(c, d, slot):
        g = turn(line, d)
        return remote(
            brows.at[rows_at(g, srows), bcols(c)],
            gback.at[rows_at(slot, srows), bcols(c)],
            gb_send.at[c, d],
            gb_recv.at[c, d],
            at(g, rank),
        )

    def b_out(c):
        return Exchange(
            "exp",
            lambda t: zback.at[rows_at(t, zrows), bcols(c)],
            lambda s: bland.at[rows_at(s, zrows), bcols(c)],
            b_send.at[c],
            b_recv.at[c],
        )

    def second_layer(c):
        def one(r):
            return jnp.dot(hidden[r], wout_land[:, bcols(c)], preferred_element_type=F32)

        far_part[:, bcols(c)] = one(across).astype(BF16)
        go(far(c, 0))
        go(far(c, 1))
        product = one(above)
        up_part[second, bcols(c)] = product[mid:].astype(BF16)
        go(near(c, 0))
        up_wait[:, bcols(c)] = product[:mid]
        product = one(below)
        down_part[first, bcols(c)] = product[:mid].astype(BF16)
        go(near(c, 1))
        down_wait[:, bcols(c)] = product[mid:]
        own_part[:, bcols(c)] = one(rank)

    def add_far(c):
        far(c, 0).wait_recv()
        up_part[first, bcols(c)] = (
            up_wait[:, bcols(c)] + half_up[:, bcols(c)].astype(F32)
        ).astype(BF16)
        go(near(c, 2))
        far(c, 1).wait_recv()
        down_part[second, bcols(c)] = (
            down_wait[:, bcols(c)] + half_down[:, bcols(c)].astype(F32)
        ).astype(BF16)
        go(near(c, 3))

    def finish(c):
        for i in (0, 1, 2, 3):
            near(c, i).wait_recv()
        brows[:, bcols(c)] = (
            own_part[:, bcols(c)]
            + full_up[:, bcols(c)].astype(F32)
            + full_down[:, bcols(c)].astype(F32)
        ).astype(BF16)
        for d in range(1, experts):
            go(from_line(c, d, line))
        gback[rows_at(line, srows), bcols(c)] = brows[rows_at(line, srows), bcols(c)]

    def give_back(c):
        for d in range(1, experts):
            from_line(c, d, turn(line, -d)).wait_recv()
        zback[:, bcols(c)] = jnp.dot(
            inverse, gback[:, bcols(c)], preferred_element_type=F32
        ).astype(BF16)
        go(b_out(c), late)
        bland[rows_at(exp, zrows), bcols(c)] = zback[rows_at(exp, zrows), bcols(c)]

    second_layer(0)
    add_far(0)
    for c in range(1, back_chunks):
        second_layer(c)
        finish(c - 1)
        add_far(c)
        give_back(c - 1)
    finish(back_chunks - 1)
    give_back(back_chunks - 1)

    q_out = Exchange(
        "seq", lambda t: qsend.at[t], lambda s: qland.at[s], q_send, q_recv
    )
    go(q_out, late)
    qland[seq] = qsend[seq]

    drain(started)
    diagonal = out_row == in_row
    gate = jnp.sum(jnp.where(diagonal, gate_ref[...], 0.0), axis=1, keepdims=True)
    for c in range(back_chunks):
        b_out(c).arrived()
        combined = lax.dot_general(
            place[...], bland[:, bcols(c)], (((0,), (0,)), ((), ())), preferred_element_type=F32
        )
        enc_out_ref[:, bcols(c)] = (enc[:, bcols(c)].astype(F32) + gate * combined).astype(BF16)
    block = rms_scale(enc_out_ref[...].astype(F32), final_gain_ref[...]).astype(BF16)
    for copy in projections:
        copy.wait()
    lane = lax.broadcasted_iota(jnp.int32, (tok, 128), 1)
    low = lane < 64
    for g in range(HEADS // 4):
        span = slice(g * 256, (g + 1) * 256)
        keys = jnp.dot(block, w_key[:, span], preferred_element_type=F32)
        values = jnp.dot(block, w_value[:, span], preferred_element_type=F32)
        for i in range(2):
            k_pair = pltpu.roll(keys[:, i * 128 : (i + 1) * 128], 64, 1)
            v_pair = values[:, i * 128 : (i + 1) * 128]
            head = g * 4 + i * 2
            kvsend[head] = jnp.where(low, v_pair, k_pair).astype(BF16)
            kvsend[head + 1] = jnp.where(low, k_pair, v_pair).astype(BF16)
    kv_out = Exchange(
        "seq",
        lambda t: kvsend.at[t],
        lambda s: kvland.at[rows_at(s, tok)],
        k_send,
        k_recv,
        route=lambda d: at(turn(line, d // experts), turn(rank, lax.rem(d, experts))),
    )
    per = n_seq // KEY_GROUPS
    kv_out.start(1, per)
    kvland[0:tok, :] = kvsend[seq]

    q_out.arrived()
    even = lax.rem(seq, 2) == 0
    q_count = 2 * q_half
    folded = qland[...].reshape(n_seq * q_half, 128).astype(F32)
    turned = pltpu.roll(folded, 64, 1)
    side = lax.broadcasted_iota(jnp.int32, folded.shape, 1)
    at_keys = jnp.where(even, side, side + 64) % 128 >= 64
    top = jnp.where(at_keys, jnp.where(even, turned, folded), 0.0).astype(BF16)
    bottom = jnp.where(at_keys, jnp.where(even, folded, turned), 0.0).astype(BF16)
    for t in range(n_seq):
        qrows[t * q_count : t * q_count + q_half, :] = top[t * q_half : (t + 1) * q_half]
        qrows[t * q_count + q_half : (t + 1) * q_count, :] = bottom[t * q_half : (t + 1) * q_half]

    drain(late)
    kv_out.loop(kv_out.send_one, 1, per)
    kv_out.start(per, n_seq)
    c_out = Exchange("seq", lambda t: csend.at[t], lambda s: cland.at[s], c_send, c_recv)
    span_rows = kvland.shape[0] // KEY_GROUPS
    wide_lane = lax.broadcasted_iota(jnp.int32, (span_rows, 128), 1)
    is_key = jnp.where(even, wide_lane, wide_lane + 64) % 128 >= 64
    pair_rows = 2 * q_count
    lane = lax.broadcasted_iota(jnp.int32, (q_half, 128), 1)
    at_values = jnp.where(even, lane, lane + 64) % 128 < 64
    group = 4

    def attend(part, last):
        span = slice(part * span_rows, (part + 1) * span_rows)
        kv_out.arrived(max(1, part * per), (part + 1) * per)
        if last:
            kv_out.loop(kv_out.send_one, per, n_seq)
        vland[span, :] = jnp.where(is_key, jnp.ones((), BF16), kvland[span, :])

        def step(d, carry):
            g = lax.rem(seq // group + d + 1, n_seq // group)
            tiles = [rows_at(2 * g + i, pair_rows) for i in range(2)]
            both = [
                lax.dot_general(
                    qrows[tile, :],
                    kvland[span, :],
                    (((1,), (1,)), ((), ())),
                    preferred_element_type=F32,
                )
                for tile in tiles
            ]
            for i, tile in enumerate(tiles):
                peak = jnp.max(both[i], axis=-1, keepdims=True)
                if part:
                    old = peaks[tile, 0:1]
                    peak = jnp.maximum(peak, old)
                expo = jnp.exp(both[i] - peak).astype(BF16)
                mixed = jnp.dot(expo, vland[span, :], preferred_element_type=F32)
                if part:
                    mixed = mixed + jnp.exp(old - peak) * sums[tile, :]
                if not last:
                    sums[tile, :] = mixed
                    peaks[tile, :] = jnp.broadcast_to(peak, mixed.shape)
                    continue
                context = mixed / pltpu.roll(mixed, 64, 1)
                turned = pltpu.roll(context, 64, 1)
                for j in range(2):
                    k = j * q_count
                    csend[g * group + 2 * i + j] = jnp.where(
                        at_values, context[k : k + q_half], turned[k + q_half : k + q_count]
                    ).astype(BF16)
            if last:
                for i in range(group):
                    t = g * group + i

                    @pl.when(t != seq)
                    def _():
                        c_out.start_one(lax.rem(t - seq + n_seq, n_seq))

            return carry

        lax.fori_loop(0, n_seq // group, step, 0, unroll=2)

    for part in range(KEY_GROUPS):
        attend(part, part == KEY_GROUPS - 1)
    cland[seq] = csend[seq]
    c_out.arrived()
    for p in range(HEADS // 2):
        one, two = cland[2 * p].astype(F32), cland[2 * p + 1].astype(F32)
        out_ref[:q_half, p * 128 : (p + 1) * 128] = jnp.where(lane < 64, one, two).astype(BF16)
        out_ref[q_half:, p * 128 : (p + 1) * 128] = pltpu.roll(
            jnp.where(lane < 64, two, one), 64, 1
        ).astype(BF16)
    c_out.wait_send()


def per_device(
    enc_in,
    expert_ids,
    slots,
    expert_gate,
    moe_gain,
    w_in,
    w_out,
    final_gain,
    w_key,
    w_value,
    dec_query,
):
    n_exp, n_seq = lax.axis_size("exp"), lax.axis_size("seq")
    tok_rows, width = enc_in.shape[1:]
    experts, _, part_ff = w_in.shape
    q_rows = dec_query.shape[1]

    vmem = pl.BlockSpec(memory_space=pltpu.VMEM)
    hbm = pl.BlockSpec(memory_space=pl.ANY)
    dma = pltpu.SemaphoreType.DMA
    whole = pltpu.VMEM((tok_rows, width), BF16)
    half = pltpu.VMEM((tok_rows // 2, width), BF16)
    weight = pltpu.VMEM((experts * part_ff, width), BF16)
    square = pltpu.VMEM((width, width), BF16)
    folded = pltpu.VMEM((n_seq, q_rows // 2, 128), BF16)
    enc_out, context = pl.pallas_call(
        layer_kernel,
        out_shape=(
            jax.ShapeDtypeStruct((tok_rows, width), BF16),
            jax.ShapeDtypeStruct((q_rows, width), BF16),
        ),
        in_specs=[hbm, vmem, vmem, vmem, vmem, hbm, hbm, vmem, hbm, hbm, hbm],
        out_specs=(vmem, vmem),
        scratch_shapes=[
            whole,
            pltpu.VMEM((q_rows, width), BF16),
            pltpu.VMEM((tok_rows, tok_rows), BF16),
            square,
            square,
            whole,
            whole,
            whole,
            pltpu.VMEM((experts, tok_rows, width), BF16),
            weight,
            weight,
            pltpu.VMEM((experts, tok_rows, experts * part_ff), BF16),
            whole,
            whole,
            whole,
            pltpu.VMEM((tok_rows // 2, width), F32),
            pltpu.VMEM((tok_rows // 2, width), F32),
            pltpu.VMEM((tok_rows, width), F32),
            half,
            half,
            whole,
            whole,
            whole,
            whole,
            whole,
            whole,
            folded,
            folded,
            pltpu.VMEM((n_seq * q_rows, 128), BF16),
            pltpu.VMEM((n_seq, tok_rows, 128), BF16),
            pltpu.VMEM((n_seq * tok_rows, 128), BF16),
            pltpu.VMEM((n_seq * tok_rows, 128), BF16),
            pltpu.VMEM((n_seq * q_rows, 128), F32),
            pltpu.VMEM((n_seq * q_rows, 128), F32),
            folded,
            folded,
            dma((6,)),
        ]
        + [dma((OUT_CHUNKS, n_exp))] * 2
        + [dma((BACK_CHUNKS, n_exp))] * 2
        + [dma((n_seq,))] * 2
        + [dma((experts,))] * 4
        + [dma((OUT_CHUNKS, experts))] * 8
        + [dma((BACK_CHUNKS, 2))] * 2
        + [dma((BACK_CHUNKS, 4))] * 2
        + [dma((BACK_CHUNKS, experts))] * 2
        + [dma((n_seq,))] * 4,
        compiler_params=pltpu.CompilerParams(
            collective_id=0, has_side_effects=True, vmem_limit_bytes=56 << 20
        ),
        name="layer",
    )(
        enc_in[0],
        expert_ids,
        slots,
        expert_gate,
        moe_gain[None],
        jnp.swapaxes(w_in, 1, 2),
        w_out,
        final_gain[None],
        w_key,
        w_value,
        dec_query[0],
    )
    return (enc_out[None], context[None])


def solution(mesh):
    placed = (
        P("exp", "seq", None),
        P("exp", "seq"),
        P("exp", "seq"),
        P("exp", "seq"),
        P(),
        P("exp", None, "seq"),
        P("exp", "seq", None),
        P(),
        P(),
        P(),
        P("exp", "seq", None),
    )
    return jax.shard_map(
        per_device,
        mesh=mesh,
        in_specs=placed,
        out_specs=(P("exp", "seq", None), P("exp", "seq", None)),
        check_vma=False,
    )
```
